32 devices in a mesh: group: 4 (over z), shard: 8 (over y, x, core).
Axes of the slice: x: 2, y: 2, z: 4, core: 2. Of those that a mesh axis runs over, the one named last changes fastest.
Arguments:
- entry_grads: float32 [4, 8, 256, 1280], P('group', 'shard'), may hold values from -800 to 800
- exit_grads: float32 [4, 8, 256, 1024], P('group', 'shard'), may hold values from -800 to 800
- entry_params: float32 [8, 256, 1280], P('shard', 'group'), may hold values from -0.15625 to 0.15625
- exit_params: float32 [8, 256, 1024], P('shard', 'group'), may hold values from -0.15625 to 0.15625
- entry_mean: float32 [8, 256, 1280], P('shard', 'group'), may hold values from -1.5 to 1.5
- exit_mean: float32 [8, 256, 1024], P('shard', 'group'), may hold values from -1.5 to 1.5
- entry_square: float32 [8, 256, 1280], P('shard', 'group'), may hold values from 0.01 to 1
- exit_square: float32 [8, 256, 1024], P('shard', 'group'), may hold values from 0.01 to 1
Outputs:
- entry_master: float32 [8, 256, 1280], P('shard', 'group')
- exit_master: float32 [8, 256, 1024], P('shard', 'group')
- entry_moment: float32 [8, 256, 1280], P('shard', 'group')
- exit_moment: float32 [8, 256, 1024], P('shard', 'group')
- entry_variance: float32 [8, 256, 1280], P('shard', 'group')
- exit_variance: float32 [8, 256, 1024], P('shard', 'group')
- entry_weights: bfloat16 [8, 256, 1280], P('shard')
- exit_weights: bfloat16 [8, 256, 1024], P('shard')
The draws below stay inside these ranges and needn't reach their ends.
All inputs are finite; a program needn't handle non-finite values.
Results may differ from the reference program's by a relative error of at most 0.0004.
Values may be sent and summed in bfloat16 or wider, within the bound.
A program may use at most 64 MiB of HBM per device.

```python
import math
import jax
import jax.numpy as jnp
from jax import lax

Q_DEV = 256
O_DEV = 256
QKV_COLS = 1280
O_COLS = 1024
GROUPS = 4
SHARDS = 8
NUMEL = 4718592


def shard_amplitude(key):
    keys = jax.random.split(key, 4)
    half_count = SHARDS // 2
    top_count = min(4, half_count)
    parity = jax.random.randint(keys[0], (), 0, 2).astype(jnp.int32)
    hot_shards = parity + 2 * jax.random.permutation(keys[1], half_count).astype(jnp.int32)
    cold_shards = 1 - parity + 2 * jax.random.permutation(keys[2], half_count).astype(jnp.int32)
    others = jax.random.permutation(keys[3], jnp.concatenate([hot_shards[top_count:], cold_shards]))
    ordering = jnp.concatenate([hot_shards[:top_count], others]).astype(jnp.int32)
    ranking = jnp.zeros((SHARDS,), jnp.int32).at[ordering].set(jnp.arange(SHARDS, dtype=jnp.int32))
    spread = ranking.astype(jnp.float32) / float(max(SHARDS - 1, 1))
    return jnp.exp(-spread * math.log(100.0))


def gradient_draw(key, rows, width):
    keys = jax.random.split(key, 5)
    shape = (GROUPS, SHARDS, rows, width)
    base = jnp.clip(jax.random.normal(keys[0], shape, jnp.float32), -6.0, 6.0)
    position = (jnp.arange(SHARDS, dtype=jnp.float32)[:, None] * rows + jnp.arange(rows, dtype=jnp.float32)[None, :]) / (SHARDS * rows)
    rising = (3.0 ** position)[None, :, :, None]
    rough = jnp.exp(jax.random.uniform(keys[1], (GROUPS, SHARDS, rows, 1), jnp.float32, 0.0, math.log(10.0)))
    column = jnp.exp(jax.random.uniform(keys[2], (1, 1, 1, width), jnp.float32, 0.0, math.log(10.0)))
    amplitude = shard_amplitude(keys[4])[None, :, None, None]
    return (base * rising * rough * column * amplitude * 0.1).astype(jnp.float32)


def draw_entry_grads(key, part):
    return gradient_draw(jax.random.fold_in(key, 11), Q_DEV, QKV_COLS)


def draw_exit_grads(key, part):
    return gradient_draw(jax.random.fold_in(key, 23), O_DEV, O_COLS)


def shard_levels(own_key, shape, pieces, least, high):
    loudness, own = 1.0, jax.random.fold_in(own_key, 6)
    for dim, shards_of in pieces:
        draws = jnp.exp(jax.random.uniform(jax.random.fold_in(own, dim), (shards_of,), jnp.float32, least / len(pieces), high / len(pieces)))
        loudness = loudness * jnp.repeat(draws, shape[dim] // shards_of).reshape([-1 if axis == dim else 1 for axis in range(len(shape))])
    return loudness


def normal_values(rng, dims, scale, most, cuts=(), kind=jnp.bfloat16):
    values = scale * jax.random.normal(rng, dims, jnp.float32)
    if cuts:
        values = values * shard_levels(rng, dims, cuts, -0.22, 0.18)
    return jnp.clip(values, -most, most).astype(kind)


def setup_inputs(seed: int = 0) -> dict:
    key_list = jax.random.split(jax.random.key(seed), 9)
    entry_grads = draw_entry_grads(jax.random.fold_in(key_list[8], 71), 0)
    exit_grads = draw_exit_grads(jax.random.fold_in(key_list[8], 71), 0)
    entry_params = normal_values(key_list[2], (SHARDS, Q_DEV, QKV_COLS), 0.01, 0.15625, ((0, 8), (1, 4)), jnp.float32)
    exit_params = normal_values(key_list[3], (SHARDS, O_DEV, O_COLS), 0.01, 0.15625, ((0, 8), (1, 4)), jnp.float32)
    entry_mean = normal_values(key_list[4], (SHARDS, Q_DEV, QKV_COLS), 0.1, 1.5, ((0, 8), (1, 4)), jnp.float32)
    exit_mean = normal_values(key_list[5], (SHARDS, O_DEV, O_COLS), 0.1, 1.5, ((0, 8), (1, 4)), jnp.float32)
    entry_square = jnp.clip(jnp.exp(math.log(1.0) - 4.6051702 * jax.random.uniform(key_list[6], (SHARDS, Q_DEV, QKV_COLS), jnp.float32) ** shard_levels(key_list[6], (SHARDS, Q_DEV, QKV_COLS), ((0, 8), (1, 4)), -0.2, 0.2)), 0.01, 1.0)
    exit_square = jnp.clip(jnp.exp(math.log(1.0) - 4.6051702 * jax.random.uniform(key_list[7], (SHARDS, O_DEV, O_COLS), jnp.float32) ** shard_levels(key_list[7], (SHARDS, O_DEV, O_COLS), ((0, 8), (1, 4)), -0.2, 0.2)), 0.01, 1.0)
    return {"entry_grads": entry_grads, "exit_grads": exit_grads, "entry_params": entry_params, "exit_params": exit_params, "entry_mean": entry_mean, "exit_mean": exit_mean, "entry_square": entry_square, "exit_square": exit_square}


beta_first = 0.9
beta_second = 0.95
learn_rate = 0.01
decay_rate = 0.1
epsilon = 1e-08
correct_first = 1.0 - 0.9 ** 40
correct_second = 1.0 - 0.95 ** 40

def adamw_step(params, mean, square, total, clip):
    grads = clip * total
    moment = beta_first * mean + (1.0 - beta_first) * grads
    variance = beta_second * square + (1.0 - beta_second) * grads * grads
    update = moment / correct_first / (jnp.sqrt(variance / correct_second) + epsilon)
    master = params - learn_rate * (update + decay_rate * params)
    return (master, moment, variance)

def reference(entry_grads, exit_grads, entry_params, exit_params, entry_mean, exit_mean, entry_square, exit_square):
    entry_total = lax.optimization_barrier(jnp.sum(entry_grads, axis=0, dtype=jnp.float32))
    exit_total = lax.optimization_barrier(jnp.sum(exit_grads, axis=0, dtype=jnp.float32))
    squares = jnp.sum(entry_total * entry_total) + jnp.sum(exit_total * exit_total)
    grad_norm = jnp.sqrt(squares)
    limit = jnp.sqrt(jnp.float32(NUMEL))
    clip = jnp.minimum(jnp.float32(1.0), limit / (grad_norm + 1e-06))
    entry_master, entry_moment, entry_variance = adamw_step(entry_params, entry_mean, entry_square, entry_total, clip)
    exit_master, exit_moment, exit_variance = adamw_step(exit_params, exit_mean, exit_square, exit_total, clip)
    return (entry_master, exit_master, entry_moment, exit_moment, entry_variance, exit_variance, entry_master.astype(jnp.bfloat16), exit_master.astype(jnp.bfloat16))
```

```python
import functools

import jax
import jax.numpy as jnp
from jax import lax
from jax.experimental import pallas as pl
from jax.experimental.pallas import tpu as pltpu
from jax.sharding import PartitionSpec as P

beta_first = 0.9
beta_second = 0.95
learn_rate = 0.01
decay_rate = 0.1
epsilon = 1e-08
correct_first = 1.0 - 0.9**40
correct_second = 1.0 - 0.95**40

MESH = pl.DeviceIdType.MESH


def adamw_step(params, mean, square, total, clip):
    grads = clip * total
    moment = beta_first * mean + (1.0 - beta_first) * grads
    variance = beta_second * square + (1.0 - beta_second) * grads * grads
    update = moment / correct_first / (jnp.sqrt(variance / correct_second) + epsilon)
    master = params - learn_rate * (update + decay_rate * params)
    return (master, moment, variance)


def squares_tile(total):
    rows, width = total.shape
    squared = total * total
    folded = squared[0:8]
    for row in range(8, rows, 8):
        folded = folded + squared[row : row + 8]
    tile = folded[:, 0:128]
    for column in range(128, width, 128):
        tile = tile + folded[:, column : column + 128]
    return tile


def kernel(
    groups,
    shards,
    count,
    pieces,
    entry_grads, exit_grads,
    entry_params, exit_params, entry_mean, exit_mean, entry_square, exit_square,
    entry_master, exit_master, entry_moment, exit_moment,
    entry_variance, exit_variance, entry_weights, exit_weights,
    entry_x, exit_x, entry_held, exit_held,
    entry_p, exit_p, entry_m, exit_m, entry_v, exit_v, entry_w, exit_w,
    group_tiles, shard_tiles,
    load_sem, state_sem, store_sem,
    sum_send, sum_recv, tile_send, tile_recv, shard_send, shard_recv,
    gather_send, gather_recv,
):
    me = lax.axis_index("group")
    shard = lax.axis_index("shard")
    kinds = 2
    grads = (entry_grads, exit_grads)
    x = (entry_x, exit_x)
    held = (entry_held, exit_held)
    states = ((entry_p, entry_m, entry_v), (exit_p, exit_m, exit_v))
    state_in = (
        (entry_params, entry_mean, entry_square),
        (exit_params, exit_mean, exit_square),
    )
    state_out = (
        (entry_master, entry_moment, entry_variance),
        (exit_master, exit_moment, exit_variance),
    )
    own_w = (entry_w, exit_w)
    weights = (entry_weights, exit_weights)
    rows = entry_p.shape[0]
    steps = groups - 1

    loads = [pltpu.make_async_copy(grads[k], x[k], load_sem.at[k]) for k in range(kinds)]
    state_loads = [
        pltpu.make_async_copy(state_in[k][i], states[k][i], state_sem.at[k, i])
        for k in range(kinds)
        for i in range(3)
    ]
    for copy in loads + state_loads:
        copy.start()

    barrier = pltpu.get_barrier_semaphore()
    for offset in range(1, groups):
        pl.semaphore_signal(
            barrier, inc=1, device_id={"group": lax.rem(me + offset, groups)}, device_id_type=MESH
        )
    for offset in range(1, shards):
        pl.semaphore_signal(
            barrier, inc=1, device_id={"shard": lax.rem(shard + offset, shards)}, device_id_type=MESH
        )
    pl.semaphore_wait(barrier, groups - 1 + shards - 1)
    for copy in loads:
        copy.wait()

    def row_block(index):
        return pl.ds(pl.multiple_of(index * rows, rows), rows)

    def place_in(stream):
        return me + stream * (groups - 1 - 2 * me)

    def peer_in(stream):
        return {"group": me + 1 - 2 * stream}

    def wanted(stream, step):
        return (groups - 1 - step) * (1 - stream) + step * stream

    def sum_copy(stream, step, k, source):
        return pltpu.make_async_remote_copy(
            src_ref=source,
            dst_ref=held[k].at[stream, step],
            send_sem=sum_send.at[stream, step, k],
            recv_sem=sum_recv.at[stream, step, k],
            device_id=peer_in(stream),
            device_id_type=MESH,
        )

    near = lax.select(me < groups // 2, 0, 1)

    @pl.when((me == 0) | (me == groups - 1))
    def _():
        order = [(step, k) for step in range(steps) for k in range(kinds)]
        copies = [
            sum_copy(near, step, k, x[k].at[row_block(wanted(near, step))]) for step, k in order
        ]
        for i, copy in enumerate(copies):
            if i >= 2:
                copies[i - 2].wait_send()
            copy.start()
        for copy in copies[-2:]:
            copy.wait_send()

    own = row_block(me)
    for step in range(steps):
        target = groups - 1 - step
        for stream in (near, 1 - near):
            place = place_in(stream)
            for k in range(kinds):

                @pl.when((place > 0) & (place <= target))
                def _(stream=stream, place=place, k=k):
                    slot = held[k].at[stream, step]
                    copy = sum_copy(stream, step, k, slot)
                    copy.wait_recv()

                    @pl.when(place < target)
                    def _():
                        slot[...] += x[k][row_block(wanted(stream, step))]
                        copy.start()

                    @pl.when(place == target)
                    def _():
                        x[k][own] += slot[...]

    group_tiles[me] = squares_tile(x[0][own]) + squares_tile(x[1][own])
    tile_copies = [
        pltpu.make_async_remote_copy(
            src_ref=group_tiles.at[me],
            dst_ref=group_tiles.at[me],
            send_sem=tile_send.at[offset],
            recv_sem=tile_recv.at[offset],
            device_id={"group": lax.rem(me + offset, groups)},
            device_id_type=MESH,
        )
        for offset in range(1, groups)
    ]
    for copy in tile_copies:
        copy.start()
    for copy in state_loads:
        copy.wait()
    for copy in tile_copies:
        copy.wait_recv()
    shard_tiles[shard] = jnp.sum(group_tiles[...], axis=0)
    shard_copies = [
        pltpu.make_async_remote_copy(
            src_ref=shard_tiles.at[shard],
            dst_ref=shard_tiles.at[shard],
            send_sem=shard_send.at[offset],
            recv_sem=shard_recv.at[offset],
            device_id={"shard": lax.rem(shard + offset, shards)},
            device_id_type=MESH,
        )
        for offset in range(1, shards)
    ]
    for copy in shard_copies:
        copy.start()
    for copy in shard_copies:
        copy.wait_recv()
    squares = jnp.sum(jnp.sum(shard_tiles[...], axis=0), keepdims=True)
    limit = jnp.sqrt(jnp.full((1, 1), count, jnp.float32))
    clip = jnp.minimum(jnp.float32(1.0), limit / (jnp.sqrt(squares) + 1e-06))

    height = rows // pieces

    def gather_copy(stream, distance, chunk, source_group, source=None):
        k, piece = chunk // pieces, chunk % pieces
        place = pl.ds(pl.multiple_of(source_group * rows + piece * height, height), height)
        return pltpu.make_async_remote_copy(
            src_ref=weights[k].at[place] if source is None else source,
            dst_ref=weights[k].at[place],
            send_sem=gather_send.at[stream, distance, chunk],
            recv_sem=gather_recv.at[stream, distance, chunk],
            device_id=peer_in(stream),
            device_id_type=MESH,
        )

    def has_next(stream):
        return me < groups - 1 if stream == 0 else me > 0

    chunks = kinds * pieces
    stores = []
    for chunk in range(chunks):
        k, piece = chunk // pieces, chunk % pieces
        part = slice(piece * height, (piece + 1) * height)
        p, m, v = states[k]
        at = pl.ds(pl.multiple_of(me * rows + piece * height, height), height)
        master, moment, variance = adamw_step(p[part], m[part], v[part], x[k][at], clip)
        own_w[k][part] = master.astype(jnp.bfloat16)
        source = own_w[k].at[part]
        for stream in range(2):

            @pl.when(has_next(stream))
            def _(stream=stream):
                gather_copy(stream, 0, chunk, me, source).start()

        p[part], m[part], v[part] = master, moment, variance
        copies = [pltpu.make_async_copy(source, weights[k].at[at], store_sem.at[chunk, 3])]
        for i in range(3):
            copies.append(
                pltpu.make_async_copy(
                    states[k][i].at[part], state_out[k][i].at[part], store_sem.at[chunk, i]
                )
            )
        for copy in copies:
            copy.start()
        stores += copies

    for distance in range(1, groups):
        for chunk in range(chunks):
            for stream in range(2):
                origin = me - distance if stream == 0 else me + distance

                @pl.when(origin >= 0 if stream == 0 else origin < groups)
                def _(stream=stream, origin=origin):
                    gather_copy(stream, distance - 1, chunk, origin).wait_recv()

                    @pl.when(has_next(stream))
                    def _():
                        gather_copy(stream, distance, chunk, origin).start()

    for distance in range(groups - 1):
        for chunk in range(chunks):
            for stream in range(2):
                origin = me - distance if stream == 0 else me + distance

                @pl.when(
                    has_next(stream) & (origin >= 0 if stream == 0 else origin < groups)
                )
                def _(stream=stream, origin=origin):
                    gather_copy(stream, distance, chunk, origin).wait_send()

    for step in range(steps):
        target = groups - 1 - step
        for stream in (near, 1 - near):
            place = place_in(stream)
            for k in range(kinds):

                @pl.when((place > 0) & (place < target))
                def _(stream=stream, k=k):
                    sum_copy(stream, step, k, held[k].at[stream, step]).wait_send()

    for copy in tile_copies + shard_copies:
        copy.wait_send()
    for copy in stores:
        copy.wait()


def body(groups, shards, *args):
    entry_grads, exit_grads, *state = args
    full, entry_width = entry_grads.shape[2:]
    exit_width = exit_grads.shape[3]
    rows = full // groups
    pieces = max(1, rows // 32)
    count = full * (entry_width + exit_width) * shards
    widths = (entry_width, exit_width)
    f32, bf16 = jnp.float32, jnp.bfloat16
    operands = [entry_grads.reshape(full, entry_width), exit_grads.reshape(full, exit_width)]
    operands += [a.reshape(a.shape[1:]) for a in state]
    small = [jax.ShapeDtypeStruct((rows, w), f32) for w in widths]
    out_shape = small * 3 + [jax.ShapeDtypeStruct((full, w), bf16) for w in widths]
    chunks = 2 * pieces
    dma = pltpu.SemaphoreType.DMA
    scratch = (
        [pltpu.VMEM((full, w), f32) for w in widths]
        + [pltpu.VMEM((2, groups - 1, rows, w), f32) for w in widths]
        + [pltpu.VMEM((rows, w), f32) for w in widths] * 3
        + [pltpu.VMEM((rows, w), bf16) for w in widths]
        + [pltpu.VMEM((groups, 8, 128), f32), pltpu.VMEM((shards, 8, 128), f32)]
        + [dma((2,)), dma((2, 3)), dma((chunks, 4))]
        + [dma((2, groups - 1, 2))] * 2
        + [dma((groups,))] * 2
        + [dma((shards,))] * 2
        + [dma((2, groups, chunks))] * 2
    )
    outs = pl.pallas_call(
        functools.partial(kernel, groups, shards, float(count), pieces),
        out_shape=out_shape,
        in_specs=[pl.BlockSpec(memory_space=pl.ANY)] * 8,
        out_specs=[pl.BlockSpec(memory_space=pl.ANY)] * 8,
        scratch_shapes=scratch,
        compiler_params=pltpu.CompilerParams(
            collective_id=0, has_side_effects=True, vmem_limit_bytes=48 * 1024 * 1024
        ),
    )(*operands)
    return tuple(a[None] for a in outs)


def solution(mesh):
    grads = P("group", "shard", None, None)
    state = P("shard", "group", None)
    gathered = P("shard", None, None)
    return jax.shard_map(
        functools.partial(body, mesh.shape["group"], mesh.shape["shard"]),
        mesh=mesh,
        in_specs=(grads,) * 2 + (state,) * 6,
        out_specs=(state,) * 6 + (gathered,) * 2,
        check_vma=False,
    )
```

```python
import functools

import jax
import jax.numpy as jnp
from jax import lax
from jax.experimental import pallas as pl
from jax.experimental.pallas import tpu as pltpu
from jax.sharding import PartitionSpec as P

beta_first = 0.9
beta_second = 0.95
learn_rate = 0.01
decay_rate = 0.1
epsilon = 1e-08
correct_first = 1.0 - 0.9**40
correct_second = 1.0 - 0.95**40

MESH = pl.DeviceIdType.MESH


def adamw_step(params, mean, square, total, clip):
    grads = clip * total
    moment = beta_first * mean + (1.0 - beta_first) * grads
    variance = beta_second * square + (1.0 - beta_second) * grads * grads
    update = moment / correct_first / (jnp.sqrt(variance / correct_second) + epsilon)
    master = params - learn_rate * (update + decay_rate * params)
    return (master, moment, variance)


def squares_tile(total):
    rows, width = total.shape
    squared = total * total
    folded = squared[0:8]
    for row in range(8, rows, 8):
        folded = folded + squared[row : row + 8]
    tile = folded[:, 0:128]
    for column in range(128, width, 128):
        tile = tile + folded[:, column : column + 128]
    return tile


def kernel(
    groups,
    shards,
    count,
    pieces,
    entry_grads, exit_grads,
    entry_params, exit_params, entry_mean, exit_mean, entry_square, exit_square,
    entry_master, exit_master, entry_moment, exit_moment,
    entry_variance, exit_variance, entry_weights, exit_weights,
    entry_x, exit_x, entry_held, exit_held,
    entry_p, exit_p, entry_m, exit_m, entry_v, exit_v, entry_w, exit_w,
    group_tiles, shard_tiles,
    load_sem, state_sem, store_sem,
    sum_send, sum_recv, tile_send, tile_recv, shard_send, shard_recv,
    gather_send, gather_recv,
):
    me = lax.axis_index("group")
    shard = lax.axis_index("shard")
    kinds = 2
    grads = (entry_grads, exit_grads)
    x = (entry_x, exit_x)
    held = (entry_held, exit_held)
    states = ((entry_p, entry_m, entry_v), (exit_p, exit_m, exit_v))
    state_in = (
        (entry_params, entry_mean, entry_square),
        (exit_params, exit_mean, exit_square),
    )
    state_out = (
        (entry_master, entry_moment, entry_variance),
        (exit_master, exit_moment, exit_variance),
    )
    own_w = (entry_w, exit_w)
    weights = (entry_weights, exit_weights)
    rows = entry_p.shape[0]
    steps = groups - 1

    loads = [pltpu.make_async_copy(grads[k], x[k], load_sem.at[k]) for k in range(kinds)]
    state_loads = [
        pltpu.make_async_copy(state_in[k][i], states[k][i], state_sem.at[k, i])
        for k in range(kinds)
        for i in range(3)
    ]
    for copy in loads + state_loads:
        copy.start()

    barrier = pltpu.get_barrier_semaphore()
    for offset in range(1, groups):
        pl.semaphore_signal(
            barrier, inc=1, device_id={"group": lax.rem(me + offset, groups)}, device_id_type=MESH
        )
    for offset in range(1, shards):
        pl.semaphore_signal(
            barrier, inc=1, device_id={"shard": lax.rem(shard + offset, shards)}, device_id_type=MESH
        )
    pl.semaphore_wait(barrier, groups - 1 + shards - 1)
    for copy in loads:
        copy.wait()

    def row_block(index):
        return pl.ds(pl.multiple_of(index * rows, rows), rows)

    def place_in(stream):
        return me + stream * (groups - 1 - 2 * me)

    def peer_in(stream):
        return {"group": me + 1 - 2 * stream}

    def wanted(stream, step):
        return (groups - 1 - step) * (1 - stream) + step * stream

    def sum_copy(stream, step, k, source):
        return pltpu.make_async_remote_copy(
            src_ref=source,
            dst_ref=held[k].at[stream, step],
            send_sem=sum_send.at[stream, step, k],
            recv_sem=sum_recv.at[stream, step, k],
            device_id=peer_in(stream),
            device_id_type=MESH,
        )

    near = lax.select(me < groups // 2, 0, 1)

    @pl.when((me == 0) | (me == groups - 1))
    def _():
        order = [(step, k) for step in range(steps) for k in range(kinds)]
        copies = [
            sum_copy(near, step, k, x[k].at[row_block(wanted(near, step))]) for step, k in order
        ]
        for i, copy in enumerate(copies):
            if i >= 2:
                copies[i - 2].wait_send()
            copy.start()
        for copy in copies[-2:]:
            copy.wait_send()

    own = row_block(me)
    for step in range(steps):
        target = groups - 1 - step
        for stream in (near, 1 - near):
            place = place_in(stream)
            for k in range(kinds):

                @pl.when((place > 0) & (place <= target))
                def _(stream=stream, place=place, k=k):
                    slot = held[k].at[stream, step]
                    copy = sum_copy(stream, step, k, slot)
                    copy.wait_recv()

                    @pl.when(place < target)
                    def _():
                        slot[...] += x[k][row_block(wanted(stream, step))]
                        copy.start()

                    @pl.when(place == target)
                    def _():
                        x[k][own] += slot[...]

    group_tiles[me] = squares_tile(x[0][own]) + squares_tile(x[1][own])
    tile_copies = [
        pltpu.make_async_remote_copy(
            src_ref=group_tiles.at[me],
            dst_ref=group_tiles.at[me],
            send_sem=tile_send.at[offset],
            recv_sem=tile_recv.at[offset],
            device_id={"group": lax.rem(me + offset, groups)},
            device_id_type=MESH,
        )
        for offset in range(1, groups)
    ]
    for copy in tile_copies:
        copy.start()
    for copy in state_loads:
        copy.wait()
    for copy in tile_copies:
        copy.wait_recv()
    shard_tiles[shard] = jnp.sum(group_tiles[...], axis=0)
    shard_copies = [
        pltpu.make_async_remote_copy(
            src_ref=shard_tiles.at[shard],
            dst_ref=shard_tiles.at[shard],
            send_sem=shard_send.at[offset],
            recv_sem=shard_recv.at[offset],
            device_id={"shard": lax.rem(shard + offset, shards)},
            device_id_type=MESH,
        )
        for offset in range(1, shards)
    ]
    for copy in shard_copies:
        copy.start()
    for copy in shard_copies:
        copy.wait_recv()
    squares = jnp.sum(jnp.sum(shard_tiles[...], axis=0), keepdims=True)
    limit = jnp.sqrt(jnp.full((1, 1), count, jnp.float32))
    clip = jnp.minimum(jnp.float32(1.0), limit / (jnp.sqrt(squares) + 1e-06))

    height = rows // pieces

    def gather_copy(stream, distance, chunk, source_group, source=None):
        k, piece = chunk // pieces, chunk % pieces
        place = pl.ds(pl.multiple_of(source_group * rows + piece * height, height), height)
        return pltpu.make_async_remote_copy(
            src_ref=weights[k].at[place] if source is None else source,
            dst_ref=weights[k].at[place],
            send_sem=gather_send.at[stream, distance, chunk],
            recv_sem=gather_recv.at[stream, distance, chunk],
            device_id=peer_in(stream),
            device_id_type=MESH,
        )

    def has_next(stream):
        return me < groups - 1 if stream == 0 else me > 0

    chunks = kinds * pieces
    stores = []
    for chunk in range(chunks):
        k, piece = chunk // pieces, chunk % pieces
        part = slice(piece * height, (piece + 1) * height)
        p, m, v = states[k]
        at = pl.ds(pl.multiple_of(me * rows + piece * height, height), height)
        master, moment, variance = adamw_step(p[part], m[part], v[part], x[k][at], clip)
        own_w[k][part] = master.astype(jnp.bfloat16)
        source = own_w[k].at[part]
        for stream in range(2):

            @pl.when(has_next(stream))
            def _(stream=stream):
                gather_copy(stream, 0, chunk, me, source).start()

        p[part], m[part], v[part] = master, moment, variance
        copies = [pltpu.make_async_copy(source, weights[k].at[at], store_sem.at[chunk, 3])]
        for i in range(3):
            copies.append(
                pltpu.make_async_copy(
                    states[k][i].at[part], state_out[k][i].at[part], store_sem.at[chunk, i]
                )
            )
        for copy in copies:
            copy.start()
        stores += copies

    for distance in range(1, groups):
        for chunk in range(chunks):
            for stream in range(2):
                origin = me - distance if stream == 0 else me + distance

                @pl.when(origin >= 0 if stream == 0 else origin < groups)
                def _(stream=stream, origin=origin):
                    gather_copy(stream, distance - 1, chunk, origin).wait_recv()

                    @pl.when(has_next(stream))
                    def _():
                        gather_copy(stream, distance, chunk, origin).start()

    for distance in range(groups - 1):
        for chunk in range(chunks):
            for stream in range(2):
                origin = me - distance if stream == 0 else me + distance

                @pl.when(
                    has_next(stream) & (origin >= 0 if stream == 0 else origin < groups)
                )
                def _(stream=stream, origin=origin):
                    gather_copy(stream, distance, chunk, origin).wait_send()

    for step in range(steps):
        target = groups - 1 - step
        for stream in (near, 1 - near):
            place = place_in(stream)
            for k in range(kinds):

                @pl.when((place > 0) & (place < target))
                def _(stream=stream, k=k):
                    sum_copy(stream, step, k, held[k].at[stream, step]).wait_send()

    for copy in tile_copies + shard_copies:
        copy.wait_send()
    for copy in stores:
        copy.wait()


def copy_kernel(*refs):
    count = len(refs) // 2
    sem = refs[-1]
    copies = [
        pltpu.make_async_copy(refs[i], refs[count + i], sem.at[i]) for i in range(count)
    ]
    for copy in copies:
        copy.start()
    for copy in copies:
        copy.wait()


def copy_out(arrays):
    moved = sum(2 * a.size * a.dtype.itemsize for a in arrays)
    return pl.pallas_call(
        copy_kernel,
        out_shape=[jax.ShapeDtypeStruct(a.shape, a.dtype) for a in arrays],
        in_specs=[pl.BlockSpec(memory_space=pltpu.HBM)] * len(arrays),
        out_specs=[pl.BlockSpec(memory_space=pltpu.HBM)] * len(arrays),
        scratch_shapes=[pltpu.SemaphoreType.DMA((len(arrays),))],
        cost_estimate=pl.CostEstimate(flops=0, bytes_accessed=moved, transcendentals=0),
        compiler_params=pltpu.CompilerParams(vmem_limit_bytes=64 * 1024 * 1024),
    )(*arrays)


def body(groups, shards, *args):
    entry_grads, exit_grads, *state = args
    full, entry_width = entry_grads.shape[2:]
    exit_width = exit_grads.shape[3]
    rows = full // groups
    pieces = max(1, rows // 32)
    count = full * (entry_width + exit_width) * shards
    widths = (entry_width, exit_width)
    f32, bf16 = jnp.float32, jnp.bfloat16
    operands = [entry_grads.reshape(full, entry_width), exit_grads.reshape(full, exit_width)]
    operands += [a.reshape(a.shape[1:]) for a in state]
    small = [jax.ShapeDtypeStruct((rows, w), f32) for w in widths]
    out_shape = small * 3 + [jax.ShapeDtypeStruct((full, w), bf16) for w in widths]
    chunks = 2 * pieces
    dma = pltpu.SemaphoreType.DMA
    scratch = (
        [pltpu.VMEM((full, w), f32) for w in widths]
        + [pltpu.VMEM((2, groups - 1, rows, w), f32) for w in widths]
        + [pltpu.VMEM((rows, w), f32) for w in widths] * 3
        + [pltpu.VMEM((rows, w), bf16) for w in widths]
        + [pltpu.VMEM((groups, 8, 128), f32), pltpu.VMEM((shards, 8, 128), f32)]
        + [dma((2,)), dma((2, 3)), dma((chunks, 4))]
        + [dma((2, groups - 1, 2))] * 2
        + [dma((groups,))] * 2
        + [dma((shards,))] * 2
        + [dma((2, groups, chunks))] * 2
    )
    outs = pl.pallas_call(
        functools.partial(kernel, groups, shards, float(count), pieces),
        out_shape=out_shape,
        in_specs=[pl.BlockSpec(memory_space=pltpu.HBM)] * 8,
        out_specs=[pl.BlockSpec(memory_space=pltpu.HBM)] * 8,
        scratch_shapes=scratch,
        compiler_params=pltpu.CompilerParams(
            collective_id=0, has_side_effects=True, vmem_limit_bytes=64 * 1024 * 1024
        ),
    )(*operands)
    return tuple(a[None] for a in copy_out(outs))


def solution(mesh):
    grads = P("group", "shard", None, None)
    state = P("shard", "group", None)
    gathered = P("shard", None, None)
    return jax.shard_map(
        functools.partial(body, mesh.shape["group"], mesh.shape["shard"]),
        mesh=mesh,
        in_specs=(grads,) * 2 + (state,) * 6,
        out_specs=(state,) * 6 + (gathered,) * 2,
        check_vma=False,
    )
```

```python
import functools

import jax
import jax.numpy as jnp
from jax import lax
from jax.experimental import pallas as pl
from jax.experimental.pallas import tpu as pltpu
from jax.sharding import PartitionSpec as P

beta_first = 0.9
beta_second = 0.95
learn_rate = 0.01
decay_rate = 0.1
epsilon = 1e-08
correct_first = 1.0 - 0.9**40
correct_second = 1.0 - 0.95**40

MESH = pl.DeviceIdType.MESH


def adamw_step(params, mean, square, total, clip):
    grads = clip * total
    moment = beta_first * mean + (1.0 - beta_first) * grads
    variance = beta_second * square + (1.0 - beta_second) * grads * grads
    update = moment / correct_first / (jnp.sqrt(variance / correct_second) + epsilon)
    master = params - learn_rate * (update + decay_rate * params)
    return (master, moment, variance)


def squares_tile(total):
    rows, width = total.shape
    squared = total * total
    folded = squared[0:8]
    for row in range(8, rows, 8):
        folded = folded + squared[row : row + 8]
    tile = folded[:, 0:128]
    for column in range(128, width, 128):
        tile = tile + folded[:, column : column + 128]
    return tile


def kernel(
    groups,
    shards,
    count,
    pieces,
    entry_grads, exit_grads,
    entry_params, exit_params, entry_mean, exit_mean, entry_square, exit_square,
    entry_master, exit_master, entry_moment, exit_moment,
    entry_variance, exit_variance, entry_weights, exit_weights,
    entry_x, exit_x, entry_held, exit_held,
    entry_p, exit_p, entry_m, exit_m, entry_v, exit_v, entry_w, exit_w,
    group_tiles, shard_tiles,
    load_sem, state_sem, store_sem, weight_sem,
    sum_send, sum_recv, tile_send, tile_recv, shard_send, shard_recv,
    gather_send, gather_recv,
):
    me = lax.axis_index("group")
    shard = lax.axis_index("shard")
    kinds = 2
    grads = (entry_grads, exit_grads)
    x = (entry_x, exit_x)
    held = (entry_held, exit_held)
    states = ((entry_p, entry_m, entry_v), (exit_p, exit_m, exit_v))
    state_in = (
        (entry_params, entry_mean, entry_square),
        (exit_params, exit_mean, exit_square),
    )
    state_out = (
        (entry_master, entry_moment, entry_variance),
        (exit_master, exit_moment, exit_variance),
    )
    gathered = (entry_w, exit_w)
    weights = (entry_weights, exit_weights)
    rows = entry_p.shape[0]
    steps = groups - 1

    loads = [pltpu.make_async_copy(grads[k], x[k], load_sem.at[k]) for k in range(kinds)]
    state_loads = [
        pltpu.make_async_copy(state_in[k][i], states[k][i], state_sem.at[k, i])
        for k in range(kinds)
        for i in range(3)
    ]
    for copy in loads + state_loads:
        copy.start()

    barrier = pltpu.get_barrier_semaphore()
    for offset in range(1, groups):
        pl.semaphore_signal(
            barrier, inc=1, device_id={"group": lax.rem(me + offset, groups)}, device_id_type=MESH
        )
    for offset in range(1, shards):
        pl.semaphore_signal(
            barrier, inc=1, device_id={"shard": lax.rem(shard + offset, shards)}, device_id_type=MESH
        )
    pl.semaphore_wait(barrier, groups - 1 + shards - 1)
    for copy in loads:
        copy.wait()

    def row_block(index):
        return pl.ds(pl.multiple_of(index * rows, rows), rows)

    def place_in(stream):
        return me + stream * (groups - 1 - 2 * me)

    def peer_in(stream):
        return {"group": me + 1 - 2 * stream}

    def wanted(stream, step):
        return (groups - 1 - step) * (1 - stream) + step * stream

    def sum_copy(stream, step, k, source):
        return pltpu.make_async_remote_copy(
            src_ref=source,
            dst_ref=held[k].at[stream, step],
            send_sem=sum_send.at[stream, step, k],
            recv_sem=sum_recv.at[stream, step, k],
            device_id=peer_in(stream),
            device_id_type=MESH,
        )

    near = lax.select(me < groups // 2, 0, 1)

    @pl.when((me == 0) | (me == groups - 1))
    def _():
        order = [(step, k) for step in range(steps) for k in range(kinds)]
        copies = [
            sum_copy(near, step, k, x[k].at[row_block(wanted(near, step))]) for step, k in order
        ]
        for i, copy in enumerate(copies):
            if i >= 2:
                copies[i - 2].wait_send()
            copy.start()
        for copy in copies[-2:]:
            copy.wait_send()

    own = row_block(me)
    for step in range(steps):
        target = groups - 1 - step
        for stream in (near, 1 - near):
            place = place_in(stream)
            for k in range(kinds):

                @pl.when((place > 0) & (place <= target))
                def _(stream=stream, place=place, k=k):
                    slot = held[k].at[stream, step]
                    copy = sum_copy(stream, step, k, slot)
                    copy.wait_recv()

                    @pl.when(place < target)
                    def _():
                        slot[...] += x[k][row_block(wanted(stream, step))]
                        copy.start()

                    @pl.when(place == target)
                    def _():
                        x[k][own] += slot[...]

    group_tiles[me] = squares_tile(x[0][own]) + squares_tile(x[1][own])
    tile_copies = [
        pltpu.make_async_remote_copy(
            src_ref=group_tiles.at[me],
            dst_ref=group_tiles.at[me],
            send_sem=tile_send.at[offset],
            recv_sem=tile_recv.at[offset],
            device_id={"group": lax.rem(me + offset, groups)},
            device_id_type=MESH,
        )
        for offset in range(1, groups)
    ]
    for copy in tile_copies:
        copy.start()
    for copy in state_loads:
        copy.wait()
    for copy in tile_copies:
        copy.wait_recv()
    shard_tiles[shard] = jnp.sum(group_tiles[...], axis=0)
    shard_copies = [
        pltpu.make_async_remote_copy(
            src_ref=shard_tiles.at[shard],
            dst_ref=shard_tiles.at[shard],
            send_sem=shard_send.at[offset],
            recv_sem=shard_recv.at[offset],
            device_id={"shard": lax.rem(shard + offset, shards)},
            device_id_type=MESH,
        )
        for offset in range(1, shards)
    ]
    for copy in shard_copies:
        copy.start()
    for copy in shard_copies:
        copy.wait_recv()
    squares = jnp.sum(jnp.sum(shard_tiles[...], axis=0), keepdims=True)
    limit = jnp.sqrt(jnp.full((1, 1), count, jnp.float32))
    clip = jnp.minimum(jnp.float32(1.0), limit / (jnp.sqrt(squares) + 1e-06))

    height = rows // pieces

    def piece_of(source_group, piece):
        return pl.ds(pl.multiple_of(source_group * rows + piece * height, height), height)

    def gather_copy(stream, distance, chunk, source_group):
        k, piece = chunk // pieces, chunk % pieces
        block = gathered[k].at[piece_of(source_group, piece)]
        return pltpu.make_async_remote_copy(
            src_ref=block,
            dst_ref=block,
            send_sem=gather_send.at[stream, distance, chunk],
            recv_sem=gather_recv.at[stream, distance, chunk],
            device_id=peer_in(stream),
            device_id_type=MESH,
        )

    def weight_store(stream, distance, chunk, source_group):
        k, piece = chunk // pieces, chunk % pieces
        place = piece_of(source_group, piece)
        return pltpu.make_async_copy(
            gathered[k].at[place], weights[k].at[place], weight_sem.at[stream, distance, chunk]
        )

    def has_next(stream):
        return me < groups - 1 if stream == 0 else me > 0

    chunks = kinds * pieces
    stores = []
    for chunk in range(chunks):
        k, piece = chunk // pieces, chunk % pieces
        part = slice(piece * height, (piece + 1) * height)
        p, m, v = states[k]
        at = piece_of(me, piece)
        master, moment, variance = adamw_step(p[part], m[part], v[part], x[k][at], clip)
        gathered[k][at] = master.astype(jnp.bfloat16)
        for stream in range(2):

            @pl.when(has_next(stream))
            def _(stream=stream):
                gather_copy(stream, 0, chunk, me).start()

        p[part], m[part], v[part] = master, moment, variance
        copies = [weight_store(0, 0, chunk, me)]
        for i in range(3):
            copies.append(
                pltpu.make_async_copy(
                    states[k][i].at[part], state_out[k][i].at[part], store_sem.at[chunk, i]
                )
            )
        for copy in copies:
            copy.start()
        stores += copies

    for distance in range(1, groups):
        for chunk in range(chunks):
            for stream in range(2):
                origin = me - distance if stream == 0 else me + distance

                @pl.when(origin >= 0 if stream == 0 else origin < groups)
                def _(stream=stream, origin=origin):
                    gather_copy(stream, distance - 1, chunk, origin).wait_recv()

                    @pl.when(has_next(stream))
                    def _():
                        gather_copy(stream, distance, chunk, origin).start()

                    weight_store(stream, distance, chunk, origin).start()

    for distance in range(groups - 1):
        for chunk in range(chunks):
            for stream in range(2):
                origin = me - distance if stream == 0 else me + distance

                @pl.when(
                    has_next(stream) & (origin >= 0 if stream == 0 else origin < groups)
                )
                def _(stream=stream, origin=origin):
                    gather_copy(stream, distance, chunk, origin).wait_send()

    for distance in range(1, groups):
        for chunk in range(chunks):
            for stream in range(2):
                origin = me - distance if stream == 0 else me + distance

                @pl.when(origin >= 0 if stream == 0 else origin < groups)
                def _(stream=stream, origin=origin):
                    weight_store(stream, distance, chunk, origin).wait()

    for step in range(steps):
        target = groups - 1 - step
        for stream in (near, 1 - near):
            place = place_in(stream)
            for k in range(kinds):

                @pl.when((place > 0) & (place < target))
                def _(stream=stream, k=k):
                    sum_copy(stream, step, k, held[k].at[stream, step]).wait_send()

    for copy in tile_copies + shard_copies:
        copy.wait_send()
    for copy in stores:
        copy.wait()


def copy_kernel(*refs):
    count = (len(refs) - 2) // 3
    ins, outs, held = refs[:count], refs[count : 2 * count], refs[2 * count : 3 * count]
    load_sem, store_sem = refs[-2:]
    loads = [pltpu.make_async_copy(ins[i], held[i], load_sem.at[i]) for i in range(count)]
    stores = [pltpu.make_async_copy(held[i], outs[i], store_sem.at[i]) for i in range(count)]
    for copy in loads:
        copy.start()
    for load, store in zip(loads, stores):
        load.wait()
        store.start()
    for copy in stores:
        copy.wait()


def copy_out(arrays):
    moved = sum(2 * a.size * a.dtype.itemsize for a in arrays)
    return pl.pallas_call(
        copy_kernel,
        out_shape=[jax.ShapeDtypeStruct(a.shape, a.dtype) for a in arrays],
        in_specs=[pl.BlockSpec(memory_space=pltpu.HBM)] * len(arrays),
        out_specs=[pl.BlockSpec(memory_space=pltpu.HBM)] * len(arrays),
        scratch_shapes=[pltpu.VMEM(a.shape, a.dtype) for a in arrays]
        + [pltpu.SemaphoreType.DMA((len(arrays),))] * 2,
        cost_estimate=pl.CostEstimate(flops=0, bytes_accessed=moved, transcendentals=0),
        compiler_params=pltpu.CompilerParams(vmem_limit_bytes=64 * 1024 * 1024),
    )(*arrays)


def body(groups, shards, *args):
    entry_grads, exit_grads, *state = args
    full, entry_width = entry_grads.shape[2:]
    exit_width = exit_grads.shape[3]
    rows = full // groups
    pieces = max(1, rows // 32)
    count = full * (entry_width + exit_width) * shards
    widths = (entry_width, exit_width)
    f32, bf16 = jnp.float32, jnp.bfloat16
    operands = [entry_grads.reshape(full, entry_width), exit_grads.reshape(full, exit_width)]
    operands += [a.reshape(a.shape[1:]) for a in state]
    small = [jax.ShapeDtypeStruct((rows, w), f32) for w in widths]
    out_shape = small * 3 + [jax.ShapeDtypeStruct((full, w), bf16) for w in widths]
    chunks = 2 * pieces
    dma = pltpu.SemaphoreType.DMA
    scratch = (
        [pltpu.VMEM((full, w), f32) for w in widths]
        + [pltpu.VMEM((2, groups - 1, rows, w), f32) for w in widths]
        + [pltpu.VMEM((rows, w), f32) for w in widths] * 3
        + [pltpu.VMEM((full, w), bf16) for w in widths]
        + [pltpu.VMEM((groups, 8, 128), f32), pltpu.VMEM((shards, 8, 128), f32)]
        + [dma((2,)), dma((2, 3)), dma((chunks, 3)), dma((2, groups, chunks))]
        + [dma((2, groups - 1, 2))] * 2
        + [dma((groups,))] * 2
        + [dma((shards,))] * 2
        + [dma((2, groups, chunks))] * 2
    )
    outs = pl.pallas_call(
        functools.partial(kernel, groups, shards, float(count), pieces),
        out_shape=out_shape,
        in_specs=[pl.BlockSpec(memory_space=pltpu.HBM)] * 8,
        out_specs=[pl.BlockSpec(memory_space=pltpu.HBM)] * 8,
        scratch_shapes=scratch,
        compiler_params=pltpu.CompilerParams(
            collective_id=0, has_side_effects=True, vmem_limit_bytes=64 * 1024 * 1024
        ),
    )(*operands)
    return tuple(a[None] for a in copy_out(outs))


def solution(mesh):
    grads = P("group", "shard", None, None)
    state = P("shard", "group", None)
    gathered = P("shard", None, None)
    return jax.shard_map(
        functools.partial(body, mesh.shape["group"], mesh.shape["shard"]),
        mesh=mesh,
        in_specs=(grads,) * 2 + (state,) * 6,
        out_specs=(state,) * 6 + (gathered,) * 2,
        check_vma=False,
    )
```

```python
import functools

import jax
import jax.numpy as jnp
from jax import lax
from jax.experimental import pallas as pl
from jax.experimental.pallas import tpu as pltpu
from jax.sharding import PartitionSpec as P

beta_first = 0.9
beta_second = 0.95
learn_rate = 0.01
decay_rate = 0.1
epsilon = 1e-08
correct_first = 1.0 - 0.9**40
correct_second = 1.0 - 0.95**40

MESH = pl.DeviceIdType.MESH


def adamw_step(params, mean, square, total, clip):
    grads = clip * total
    moment = beta_first * mean + (1.0 - beta_first) * grads
    variance = beta_second * square + (1.0 - beta_second) * grads * grads
    update = moment / correct_first / (jnp.sqrt(variance / correct_second) + epsilon)
    master = params - learn_rate * (update + decay_rate * params)
    return (master, moment, variance)


def squares_tile(total):
    rows, width = total.shape
    squared = total * total
    folded = squared[0:8]
    for row in range(8, rows, 8):
        folded = folded + squared[row : row + 8]
    tile = folded[:, 0:128]
    for column in range(128, width, 128):
        tile = tile + folded[:, column : column + 128]
    return tile


def kernel(
    groups,
    shards,
    count,
    pieces,
    entry_grads, exit_grads,
    entry_params, exit_params, entry_mean, exit_mean, entry_square, exit_square,
    entry_master, exit_master, entry_moment, exit_moment,
    entry_variance, exit_variance, entry_weights, exit_weights,
    entry_x, exit_x, entry_held, exit_held,
    entry_p, exit_p, entry_m, exit_m, entry_v, exit_v, entry_w, exit_w,
    group_tiles, shard_tiles,
    load_sem, state_sem, store_sem, weight_sem,
    sum_send, sum_recv, tile_send, tile_recv, shard_send, shard_recv,
    gather_send, gather_recv,
):
    me = lax.axis_index("group")
    shard = lax.axis_index("shard")
    kinds = 2
    grads = (entry_grads, exit_grads)
    x = (entry_x, exit_x)
    held = (entry_held, exit_held)
    states = ((entry_p, entry_m, entry_v), (exit_p, exit_m, exit_v))
    state_in = (
        (entry_params, entry_mean, entry_square),
        (exit_params, exit_mean, exit_square),
    )
    state_out = (
        (entry_master, entry_moment, entry_variance),
        (exit_master, exit_moment, exit_variance),
    )
    gathered = (entry_w, exit_w)
    weights = (entry_weights, exit_weights)
    rows = entry_p.shape[0]
    steps = groups - 1

    def row_block(index):
        return pl.ds(pl.multiple_of(index * rows, rows), rows)

    near = lax.select(me < groups // 2, 0, 1)

    def wanted(stream, step):
        return (groups - 1 - step) * (1 - stream) + step * stream

    def load(k, step):
        block = row_block(wanted(near, step))
        return pltpu.make_async_copy(grads[k].at[block], x[k].at[block], load_sem.at[step, k])

    for step in range(groups):
        for k in range(kinds):
            load(k, step).start()

    barrier = pltpu.get_barrier_semaphore()
    for offset in range(1, groups):
        pl.semaphore_signal(
            barrier, inc=1, device_id={"group": lax.rem(me + offset, groups)}, device_id_type=MESH
        )
    for offset in range(1, shards):
        pl.semaphore_signal(
            barrier, inc=1, device_id={"shard": lax.rem(shard + offset, shards)}, device_id_type=MESH
        )
    pl.semaphore_wait(barrier, groups - 1 + shards - 1)
    state_loads = [
        pltpu.make_async_copy(state_in[k][i], states[k][i], state_sem.at[k, i])
        for k in range(kinds)
        for i in range(3)
    ]
    for copy in state_loads:
        copy.start()

    height = rows // pieces
    chunks = kinds * pieces

    def place_in(stream):
        return me + stream * (groups - 1 - 2 * me)

    def peer_in(stream):
        return {"group": me + 1 - 2 * stream}

    def piece_of(block, piece):
        return pl.ds(pl.multiple_of(block * rows + piece * height, height), height)

    def slot_of(stream, step, chunk):
        k, piece = chunk // pieces, chunk % pieces
        return held[k].at[stream, step, slice(piece * height, (piece + 1) * height)]

    def sum_copy(stream, step, chunk, source):
        return pltpu.make_async_remote_copy(
            src_ref=source,
            dst_ref=slot_of(stream, step, chunk),
            send_sem=sum_send.at[stream, step, chunk],
            recv_sem=sum_recv.at[stream, step, chunk],
            device_id=peer_in(stream),
            device_id_type=MESH,
        )

    @pl.when((me == 0) | (me == groups - 1))
    def _():
        copies = []
        for step in range(steps):
            for chunk in range(chunks):
                k, piece = chunk // pieces, chunk % pieces
                if piece == 0:
                    load(k, step).wait()
                source = x[k].at[piece_of(wanted(near, step), piece)]
                copies.append(sum_copy(near, step, chunk, source))
                if len(copies) > 2:
                    copies[-3].wait_send()
                copies[-1].start()
        for copy in copies[-2:]:
            copy.wait_send()

    @pl.when((me > 0) & (me < groups - 1))
    def _():
        for step in range(steps):
            for k in range(kinds):
                load(k, step).wait()

    for k in range(kinds):
        load(k, steps).wait()

    own = row_block(me)
    for step in range(steps):
        target = groups - 1 - step
        for stream in (near, 1 - near):
            place = place_in(stream)
            for chunk in range(chunks):
                k, piece = chunk // pieces, chunk % pieces

                @pl.when((place > 0) & (place <= target))
                def _(stream=stream, place=place, k=k, piece=piece, chunk=chunk):
                    slot = slot_of(stream, step, chunk)
                    copy = sum_copy(stream, step, chunk, slot)
                    copy.wait_recv()

                    @pl.when(place < target)
                    def _():
                        slot[...] += x[k][piece_of(wanted(stream, step), piece)]
                        copy.start()

                    @pl.when(place == target)
                    def _():
                        x[k][piece_of(me, piece)] += slot[...]

    group_tiles[me] = squares_tile(x[0][own]) + squares_tile(x[1][own])
    tile_copies = [
        pltpu.make_async_remote_copy(
            src_ref=group_tiles.at[me],
            dst_ref=group_tiles.at[me],
            send_sem=tile_send.at[offset],
            recv_sem=tile_recv.at[offset],
            device_id={"group": lax.rem(me + offset, groups)},
            device_id_type=MESH,
        )
        for offset in range(1, groups)
    ]
    for copy in tile_copies:
        copy.start()
    for copy in state_loads:
        copy.wait()
    for copy in tile_copies:
        copy.wait_recv()
    shard_tiles[shard] = jnp.sum(group_tiles[...], axis=0)
    shard_copies = [
        pltpu.make_async_remote_copy(
            src_ref=shard_tiles.at[shard],
            dst_ref=shard_tiles.at[shard],
            send_sem=shard_send.at[offset],
            recv_sem=shard_recv.at[offset],
            device_id={"shard": lax.rem(shard + offset, shards)},
            device_id_type=MESH,
        )
        for offset in range(1, shards)
    ]
    for copy in shard_copies:
        copy.start()
    for copy in shard_copies:
        copy.wait_recv()
    squares = jnp.sum(jnp.sum(shard_tiles[...], axis=0), keepdims=True)
    limit = jnp.sqrt(jnp.full((1, 1), count, jnp.float32))
    clip = jnp.minimum(jnp.float32(1.0), limit / (jnp.sqrt(squares) + 1e-06))

    def gather_copy(stream, distance, chunk, source_group):
        k, piece = chunk // pieces, chunk % pieces
        block = gathered[k].at[piece_of(source_group, piece)]
        return pltpu.make_async_remote_copy(
            src_ref=block,
            dst_ref=block,
            send_sem=gather_send.at[stream, distance, chunk],
            recv_sem=gather_recv.at[stream, distance, chunk],
            device_id=peer_in(stream),
            device_id_type=MESH,
        )

    def weight_store(stream, distance, chunk, source_group):
        k, piece = chunk // pieces, chunk % pieces
        place = piece_of(source_group, piece)
        return pltpu.make_async_copy(
            gathered[k].at[place], weights[k].at[place], weight_sem.at[stream, distance, chunk]
        )

    def has_next(stream):
        return me < groups - 1 if stream == 0 else me > 0

    stores = []
    for chunk in range(chunks):
        k, piece = chunk // pieces, chunk % pieces
        part = slice(piece * height, (piece + 1) * height)
        p, m, v = states[k]
        at = piece_of(me, piece)
        master, moment, variance = adamw_step(p[part], m[part], v[part], x[k][at], clip)
        gathered[k][at] = master.astype(jnp.bfloat16)
        for stream in range(2):

            @pl.when(has_next(stream))
            def _(stream=stream):
                if chunk >= 2:
                    gather_copy(stream, 0, chunk - 2, me).wait_send()
                gather_copy(stream, 0, chunk, me).start()

        p[part], m[part], v[part] = master, moment, variance
        copies = [weight_store(0, 0, chunk, me)]
        for i in range(3):
            copies.append(
                pltpu.make_async_copy(
                    states[k][i].at[part], state_out[k][i].at[part], store_sem.at[chunk, i]
                )
            )
        for copy in copies:
            copy.start()
        stores += copies

    for distance in range(1, groups):
        for chunk in range(chunks):
            for stream in range(2):
                origin = me - distance if stream == 0 else me + distance

                @pl.when(origin >= 0 if stream == 0 else origin < groups)
                def _(stream=stream, origin=origin):
                    gather_copy(stream, distance - 1, chunk, origin).wait_recv()

                    @pl.when(has_next(stream))
                    def _():
                        gather_copy(stream, distance, chunk, origin).start()

                    weight_store(stream, distance, chunk, origin).start()

    for distance in range(groups - 1):
        for chunk in range(0 if distance else chunks - 2, chunks):
            for stream in range(2):
                origin = me - distance if stream == 0 else me + distance

                @pl.when(
                    has_next(stream) & (origin >= 0 if stream == 0 else origin < groups)
                )
                def _(stream=stream, origin=origin):
                    gather_copy(stream, distance, chunk, origin).wait_send()

    for distance in range(1, groups):
        for chunk in range(chunks):
            for stream in range(2):
                origin = me - distance if stream == 0 else me + distance

                @pl.when(origin >= 0 if stream == 0 else origin < groups)
                def _(stream=stream, origin=origin):
                    weight_store(stream, distance, chunk, origin).wait()

    for step in range(steps):
        target = groups - 1 - step
        for stream in (near, 1 - near):
            place = place_in(stream)
            for chunk in range(chunks):

                @pl.when((place > 0) & (place < target))
                def _(stream=stream, chunk=chunk):
                    sum_copy(stream, step, chunk, slot_of(stream, step, chunk)).wait_send()

    for copy in tile_copies + shard_copies:
        copy.wait_send()
    for copy in stores:
        copy.wait()


def copy_kernel(*refs):
    count = (len(refs) - 2) // 3
    ins, outs, held = refs[:count], refs[count : 2 * count], refs[2 * count : 3 * count]
    load_sem, store_sem = refs[-2:]
    loads = [pltpu.make_async_copy(ins[i], held[i], load_sem.at[i]) for i in range(count)]
    stores = [pltpu.make_async_copy(held[i], outs[i], store_sem.at[i]) for i in range(count)]
    for copy in loads:
        copy.start()
    for load, store in zip(loads, stores):
        load.wait()
        store.start()
    for copy in stores:
        copy.wait()


def copy_out(arrays):
    moved = sum(2 * a.size * a.dtype.itemsize for a in arrays)
    return pl.pallas_call(
        copy_kernel,
        out_shape=[jax.ShapeDtypeStruct(a.shape, a.dtype) for a in arrays],
        in_specs=[pl.BlockSpec(memory_space=pltpu.HBM)] * len(arrays),
        out_specs=[pl.BlockSpec(memory_space=pltpu.HBM)] * len(arrays),
        scratch_shapes=[pltpu.VMEM(a.shape, a.dtype) for a in arrays]
        + [pltpu.SemaphoreType.DMA((len(arrays),))] * 2,
        cost_estimate=pl.CostEstimate(flops=0, bytes_accessed=moved, transcendentals=0),
        compiler_params=pltpu.CompilerParams(vmem_limit_bytes=64 * 1024 * 1024),
    )(*arrays)


def body(groups, shards, *args):
    entry_grads, exit_grads, *state = args
    full, entry_width = entry_grads.shape[2:]
    exit_width = exit_grads.shape[3]
    rows = full // groups
    pieces = max(1, rows // 32)
    count = full * (entry_width + exit_width) * shards
    widths = (entry_width, exit_width)
    f32, bf16 = jnp.float32, jnp.bfloat16
    operands = [entry_grads.reshape(full, entry_width), exit_grads.reshape(full, exit_width)]
    operands += [a.reshape(a.shape[1:]) for a in state]
    small = [jax.ShapeDtypeStruct((rows, w), f32) for w in widths]
    out_shape = small * 3 + [jax.ShapeDtypeStruct((full, w), bf16) for w in widths]
    chunks = 2 * pieces
    dma = pltpu.SemaphoreType.DMA
    scratch = (
        [pltpu.VMEM((full, w), f32) for w in widths]
        + [pltpu.VMEM((2, groups - 1, rows, w), f32) for w in widths]
        + [pltpu.VMEM((rows, w), f32) for w in widths] * 3
        + [pltpu.VMEM((full, w), bf16) for w in widths]
        + [pltpu.VMEM((groups, 8, 128), f32), pltpu.VMEM((shards, 8, 128), f32)]
        + [dma((groups, 2)), dma((2, 3)), dma((chunks, 3)), dma((2, groups, chunks))]
        + [dma((2, groups - 1, chunks))] * 2
        + [dma((groups,))] * 2
        + [dma((shards,))] * 2
        + [dma((2, groups, chunks))] * 2
    )
    outs = pl.pallas_call(
        functools.partial(kernel, groups, shards, float(count), pieces),
        out_shape=out_shape,
        in_specs=[pl.BlockSpec(memory_space=pltpu.HBM)] * 8,
        out_specs=[pl.BlockSpec(memory_space=pltpu.HBM)] * 8,
        scratch_shapes=scratch,
        compiler_params=pltpu.CompilerParams(
            collective_id=0, has_side_effects=True, vmem_limit_bytes=64 * 1024 * 1024
        ),
    )(*operands)
    return tuple(a[None] for a in copy_out(outs))


def solution(mesh):
    grads = P("group", "shard", None, None)
    state = P("shard", "group", None)
    gathered = P("shard", None, None)
    return jax.shard_map(
        functools.partial(body, mesh.shape["group"], mesh.shape["shard"]),
        mesh=mesh,
        in_specs=(grads,) * 2 + (state,) * 6,
        out_specs=(state,) * 6 + (gathered,) * 2,
        check_vma=False,
    )
```

```python
import functools

import jax
import jax.numpy as jnp
from jax import lax
from jax.experimental import pallas as pl
from jax.experimental.pallas import tpu as pltpu
from jax.sharding import PartitionSpec as P

beta_first = 0.9
beta_second = 0.95
learn_rate = 0.01
decay_rate = 0.1
epsilon = 1e-08
correct_first = 1.0 - 0.9**40
correct_second = 1.0 - 0.95**40

MESH = pl.DeviceIdType.MESH


def adamw_step(params, mean, square, total, clip):
    grads = clip * total
    moment = beta_first * mean + (1.0 - beta_first) * grads
    variance = beta_second * square + (1.0 - beta_second) * grads * grads
    update = moment / correct_first / (jnp.sqrt(variance / correct_second) + epsilon)
    master = params - learn_rate * (update + decay_rate * params)
    return (master, moment, variance)


def squares_tile(total):
    rows, width = total.shape
    squared = total * total
    folded = squared[0:8]
    for row in range(8, rows, 8):
        folded = folded + squared[row : row + 8]
    tile = folded[:, 0:128]
    for column in range(128, width, 128):
        tile = tile + folded[:, column : column + 128]
    return tile


def kernel(
    groups,
    shards,
    count,
    pieces,
    entry_grads, exit_grads,
    entry_params, exit_params, entry_mean, exit_mean, entry_square, exit_square,
    entry_master, exit_master, entry_moment, exit_moment,
    entry_variance, exit_variance, entry_weights, exit_weights,
    entry_x, exit_x, entry_held, exit_held,
    entry_p, exit_p, entry_m, exit_m, entry_v, exit_v, entry_w, exit_w,
    group_tiles, shard_tiles,
    load_sem, state_sem, store_sem, weight_sem,
    sum_send, sum_recv, tile_send, tile_recv, shard_send, shard_recv,
    gather_send, gather_recv,
):
    me = lax.axis_index("group")
    shard = lax.axis_index("shard")
    kinds = 2
    grads = (entry_grads, exit_grads)
    x = (entry_x, exit_x)
    held = (entry_held, exit_held)
    states = ((entry_p, entry_m, entry_v), (exit_p, exit_m, exit_v))
    state_in = (
        (entry_params, entry_mean, entry_square),
        (exit_params, exit_mean, exit_square),
    )
    state_out = (
        (entry_master, entry_moment, entry_variance),
        (exit_master, exit_moment, exit_variance),
    )
    gathered = (entry_w, exit_w)
    weights = (entry_weights, exit_weights)
    rows = entry_p.shape[0]
    steps = groups - 1

    def row_block(index):
        return pl.ds(pl.multiple_of(index * rows, rows), rows)

    near = lax.select(me < groups // 2, 0, 1)

    def wanted(stream, step):
        return (groups - 1 - step) * (1 - stream) + step * stream

    def load(k, step):
        block = row_block(wanted(near, step))
        return pltpu.make_async_copy(grads[k].at[block], x[k].at[block], load_sem.at[step, k])

    for step in range(groups):
        for k in range(kinds):
            load(k, step).start()

    barrier = pltpu.get_barrier_semaphore()
    for offset in range(1, groups):
        pl.semaphore_signal(
            barrier, inc=1, device_id={"group": lax.rem(me + offset, groups)}, device_id_type=MESH
        )
    for offset in range(1, shards):
        pl.semaphore_signal(
            barrier, inc=1, device_id={"shard": lax.rem(shard + offset, shards)}, device_id_type=MESH
        )
    pl.semaphore_wait(barrier, groups - 1 + shards - 1)
    state_loads = [
        pltpu.make_async_copy(state_in[k][i], states[k][i], state_sem.at[k, i])
        for k in range(kinds)
        for i in range(3)
    ]
    for copy in state_loads:
        copy.start()

    height = rows // pieces
    chunks = kinds * pieces

    def place_in(stream):
        return me + stream * (groups - 1 - 2 * me)

    def peer_in(stream):
        return {"group": me + 1 - 2 * stream}

    def piece_of(block, piece):
        return pl.ds(pl.multiple_of(block * rows + piece * height, height), height)

    def slot_of(stream, step, chunk):
        k, piece = chunk // pieces, chunk % pieces
        return held[k].at[stream, step, slice(piece * height, (piece + 1) * height)]

    def sum_copy(stream, step, chunk, source):
        return pltpu.make_async_remote_copy(
            src_ref=source,
            dst_ref=slot_of(stream, step, chunk),
            send_sem=sum_send.at[stream, step, chunk],
            recv_sem=sum_recv.at[stream, step, chunk],
            device_id=peer_in(stream),
            device_id_type=MESH,
        )

    if groups == 4:
        is_end = (me == 0) | (me == 3)
        mirror = me // 2
        total = 2 * chunks

        def block(j):
            return j + mirror * (3 - 2 * j)

        inwards = {"group": me + 1 - 2 * mirror}
        outwards = {"group": me - 1 + 2 * mirror}

        def line_copy(source, send, lane, step, chunk, peer):
            return pltpu.make_async_remote_copy(
                src_ref=source,
                dst_ref=slot_of(lane, step, chunk),
                send_sem=sum_send.at[send, step, chunk],
                recv_sem=sum_recv.at[lane, step, chunk],
                device_id=peer,
                device_id_type=MESH,
            )

        def end_copy(n):
            step, chunk = n // chunks, n % chunks
            source = x[chunk // pieces].at[piece_of(block(3 - step), chunk % pieces)]
            return line_copy(source, 0, 0, step, chunk, inwards)

        def across_copy(n):
            step, chunk = n // chunks, n % chunks
            return line_copy(slot_of(0, step, chunk), 0, 1, step, chunk, inwards)

        def back_copy(n):
            step, chunk = n // chunks, n % chunks
            return line_copy(slot_of(1, step, chunk), 1, 1, step, chunk, outwards)

        def shard_copy(offset):
            return pltpu.make_async_remote_copy(
                src_ref=shard_tiles.at[shard],
                dst_ref=shard_tiles.at[shard],
                send_sem=shard_send.at[offset],
                recv_sem=shard_recv.at[offset],
                device_id={"shard": lax.rem(shard + offset, shards)},
                device_id_type=MESH,
            )

        def tile_copy(offset):
            return pltpu.make_async_remote_copy(
                src_ref=group_tiles.at[me],
                dst_ref=group_tiles.at[me],
                send_sem=tile_send.at[offset],
                recv_sem=tile_recv.at[offset],
                device_id={"group": lax.rem(me + offset, groups)},
                device_id_type=MESH,
            )

        @pl.when(is_end)
        def _():
            lag = 6
            shard_tiles[shard] = jnp.zeros((8, 128), jnp.float32)
            for n in range(total + max(chunks, lag)):
                if n == 0:
                    load(0, 0).wait()
                if n == 1:
                    for step in range(groups):
                        for k in range(kinds):
                            if (step, k) != (0, 0):
                                load(k, step).wait()
                if n < total + chunks:
                    if n >= 2:
                        end_copy(n - 2).wait_send()
                    end_copy(n).start()
                m = n - lag
                if 0 <= m < total:
                    step, chunk = m // chunks, m % chunks
                    k, place = chunk // pieces, piece_of(block(step), chunk % pieces)
                    back_copy(m).wait_recv()
                    summed = x[k][place] + slot_of(1, step, chunk)[...]
                    if step == 0:
                        x[k][place] = summed
                    shard_tiles[shard] += squares_tile(summed)
                if m == total - 1:
                    for offset in range(1, shards):
                        shard_copy(offset).start()
            for offset in range(1, shards):
                shard_copy(offset).wait_recv()
            group_tiles[me] = jnp.sum(shard_tiles[...], axis=0)
            for offset in range(1, groups):
                tile_copy(offset).start()

        @pl.when(jnp.logical_not(is_end))
        def _():
            for step in range(groups):
                for k in range(kinds):
                    load(k, step).wait()
            for n in range(total + 1):
                if n < total:
                    step, chunk = n // chunks, n % chunks
                    k, place = chunk // pieces, piece_of(block(3 - step), chunk % pieces)
                    end_copy(n).wait_recv()
                    slot_of(0, step, chunk)[...] += x[k][place]
                    across_copy(n).start()
                if n >= 1:
                    step, chunk = (n - 1) // chunks, (n - 1) % chunks
                    k, place = chunk // pieces, piece_of(block(step), chunk % pieces)
                    across_copy(n - 1).wait_recv()
                    slot_of(1, step, chunk)[...] += x[k][place]
                    back_copy(n - 1).start()

        for copy in state_loads:
            copy.wait()
        for source in (0, 3):

            @pl.when(me != source)
            def _(source=source):
                tile_copy(lax.rem(me - source + groups, groups)).wait_recv()

        norm_tiles = jnp.stack([group_tiles[0], group_tiles[3]])
    else:
        @pl.when((me == 0) | (me == groups - 1))
        def _():
            copies = []
            for step in range(steps):
                for chunk in range(chunks):
                    k, piece = chunk // pieces, chunk % pieces
                    if piece == 0:
                        load(k, step).wait()
                    source = x[k].at[piece_of(wanted(near, step), piece)]
                    copies.append(sum_copy(near, step, chunk, source))
                    if len(copies) > 2:
                        copies[-3].wait_send()
                    copies[-1].start()
            for copy in copies[-2:]:
                copy.wait_send()

        @pl.when((me > 0) & (me < groups - 1))
        def _():
            for step in range(steps):
                for k in range(kinds):
                    load(k, step).wait()

        for k in range(kinds):
            load(k, steps).wait()

        own = row_block(me)
        for step in range(steps):
            target = groups - 1 - step
            for stream in (near, 1 - near):
                place = place_in(stream)
                for chunk in range(chunks):
                    k, piece = chunk // pieces, chunk % pieces

                    @pl.when((place > 0) & (place <= target))
                    def _(stream=stream, place=place, k=k, piece=piece, chunk=chunk):
                        slot = slot_of(stream, step, chunk)
                        copy = sum_copy(stream, step, chunk, slot)
                        copy.wait_recv()

                        @pl.when(place < target)
                        def _():
                            slot[...] += x[k][piece_of(wanted(stream, step), piece)]
                            copy.start()

                        @pl.when(place == target)
                        def _():
                            x[k][piece_of(me, piece)] += slot[...]

        group_tiles[me] = squares_tile(x[0][own]) + squares_tile(x[1][own])
        tile_copies = [
            pltpu.make_async_remote_copy(
                src_ref=group_tiles.at[me],
                dst_ref=group_tiles.at[me],
                send_sem=tile_send.at[offset],
                recv_sem=tile_recv.at[offset],
                device_id={"group": lax.rem(me + offset, groups)},
                device_id_type=MESH,
            )
            for offset in range(1, groups)
        ]
        for copy in tile_copies:
            copy.start()
        for copy in tile_copies:
            copy.wait_recv()
        shard_tiles[shard] = jnp.sum(group_tiles[...], axis=0)
        shard_copies = [
            pltpu.make_async_remote_copy(
                src_ref=shard_tiles.at[shard],
                dst_ref=shard_tiles.at[shard],
                send_sem=shard_send.at[offset],
                recv_sem=shard_recv.at[offset],
                device_id={"shard": lax.rem(shard + offset, shards)},
                device_id_type=MESH,
            )
            for offset in range(1, shards)
        ]
        for copy in shard_copies:
            copy.start()
        for copy in shard_copies:
            copy.wait_recv()
        norm_tiles = shard_tiles[...]
        for copy in state_loads:
            copy.wait()

    squares = jnp.sum(jnp.sum(norm_tiles, axis=0), keepdims=True)
    limit = jnp.sqrt(jnp.full((1, 1), count, jnp.float32))
    clip = jnp.minimum(jnp.float32(1.0), limit / (jnp.sqrt(squares) + 1e-06))

    def gather_copy(stream, distance, chunk, source_group):
        k, piece = chunk // pieces, chunk % pieces
        block = gathered[k].at[piece_of(source_group, piece)]
        return pltpu.make_async_remote_copy(
            src_ref=block,
            dst_ref=block,
            send_sem=gather_send.at[stream, distance, chunk],
            recv_sem=gather_recv.at[stream, distance, chunk],
            device_id=peer_in(stream),
            device_id_type=MESH,
        )

    def weight_store(stream, distance, chunk, source_group):
        k, piece = chunk // pieces, chunk % pieces
        place = piece_of(source_group, piece)
        return pltpu.make_async_copy(
            gathered[k].at[place], weights[k].at[place], weight_sem.at[stream, distance, chunk]
        )

    def has_next(stream):
        return me < groups - 1 if stream == 0 else me > 0

    stores = []
    for chunk in range(chunks):
        k, piece = chunk // pieces, chunk % pieces
        part = slice(piece * height, (piece + 1) * height)
        p, m, v = states[k]
        at = piece_of(me, piece)
        if groups == 4:

            @pl.when(jnp.logical_not(is_end))
            def _():
                end_copy(total + chunk).wait_recv()
                x[k][at] = slot_of(1, 1, chunk)[...] + slot_of(0, 2, chunk)[...]

        master, moment, variance = adamw_step(p[part], m[part], v[part], x[k][at], clip)
        gathered[k][at] = master.astype(jnp.bfloat16)
        for stream in range(2):

            @pl.when(has_next(stream))
            def _(stream=stream):
                if chunk >= 3:
                    gather_copy(stream, 0, chunk - 3, me).wait_send()
                gather_copy(stream, 0, chunk, me).start()

        p[part], m[part], v[part] = master, moment, variance
        copies = [weight_store(0, 0, chunk, me)]
        for i in range(3):
            copies.append(
                pltpu.make_async_copy(
                    states[k][i].at[part], state_out[k][i].at[part], store_sem.at[chunk, i]
                )
            )
        for copy in copies:
            copy.start()
        stores += copies

    for distance in range(1, groups):
        for chunk in range(chunks):
            for stream in range(2):
                origin = me - distance if stream == 0 else me + distance

                @pl.when(origin >= 0 if stream == 0 else origin < groups)
                def _(stream=stream, origin=origin):
                    gather_copy(stream, distance - 1, chunk, origin).wait_recv()

                    @pl.when(has_next(stream))
                    def _():
                        gather_copy(stream, distance, chunk, origin).start()

                    weight_store(stream, distance, chunk, origin).start()

    for distance in range(groups - 1):
        for chunk in range(0 if distance else max(0, chunks - 3), chunks):
            for stream in range(2):
                origin = me - distance if stream == 0 else me + distance

                @pl.when(
                    has_next(stream) & (origin >= 0 if stream == 0 else origin < groups)
                )
                def _(stream=stream, origin=origin):
                    gather_copy(stream, distance, chunk, origin).wait_send()

    for distance in range(1, groups):
        for chunk in range(chunks):
            for stream in range(2):
                origin = me - distance if stream == 0 else me + distance

                @pl.when(origin >= 0 if stream == 0 else origin < groups)
                def _(stream=stream, origin=origin):
                    weight_store(stream, distance, chunk, origin).wait()

    if groups == 4:

        @pl.when(is_end)
        def _():
            for n in range(total + chunks - 2, total + chunks):
                end_copy(n).wait_send()
            for offset in range(1, shards):
                shard_copy(offset).wait_send()
            for offset in range(1, groups):
                tile_copy(offset).wait_send()

        @pl.when(jnp.logical_not(is_end))
        def _():
            for n in range(total):
                across_copy(n).wait_send()
                back_copy(n).wait_send()

    else:
        for step in range(steps):
            target = groups - 1 - step
            for stream in (near, 1 - near):
                place = place_in(stream)
                for chunk in range(chunks):

                    @pl.when((place > 0) & (place < target))
                    def _(stream=stream, chunk=chunk):
                        sum_copy(stream, step, chunk, slot_of(stream, step, chunk)).wait_send()

        for copy in tile_copies + shard_copies:
            copy.wait_send()
    for copy in stores:
        copy.wait()


def copy_kernel(*refs):
    count = (len(refs) - 2) // 3
    ins, outs, held = refs[:count], refs[count : 2 * count], refs[2 * count : 3 * count]
    load_sem, store_sem = refs[-2:]
    loads = [pltpu.make_async_copy(ins[i], held[i], load_sem.at[i]) for i in range(count)]
    stores = [pltpu.make_async_copy(held[i], outs[i], store_sem.at[i]) for i in range(count)]
    for copy in loads:
        copy.start()
    for load, store in zip(loads, stores):
        load.wait()
        store.start()
    for copy in stores:
        copy.wait()


def copy_out(arrays):
    moved = sum(2 * a.size * a.dtype.itemsize for a in arrays)
    return pl.pallas_call(
        copy_kernel,
        out_shape=[jax.ShapeDtypeStruct(a.shape, a.dtype) for a in arrays],
        in_specs=[pl.BlockSpec(memory_space=pltpu.HBM)] * len(arrays),
        out_specs=[pl.BlockSpec(memory_space=pltpu.HBM)] * len(arrays),
        scratch_shapes=[pltpu.VMEM(a.shape, a.dtype) for a in arrays]
        + [pltpu.SemaphoreType.DMA((len(arrays),))] * 2,
        cost_estimate=pl.CostEstimate(flops=0, bytes_accessed=moved, transcendentals=0),
        compiler_params=pltpu.CompilerParams(vmem_limit_bytes=64 * 1024 * 1024),
    )(*arrays)


def body(groups, shards, *args):
    entry_grads, exit_grads, *state = args
    full, entry_width = entry_grads.shape[2:]
    exit_width = exit_grads.shape[3]
    rows = full // groups
    pieces = max(1, rows // 16)
    count = full * (entry_width + exit_width) * shards
    widths = (entry_width, exit_width)
    f32, bf16 = jnp.float32, jnp.bfloat16
    operands = [entry_grads.reshape(full, entry_width), exit_grads.reshape(full, exit_width)]
    operands += [a.reshape(a.shape[1:]) for a in state]
    small = [jax.ShapeDtypeStruct((rows, w), f32) for w in widths]
    out_shape = small * 3 + [jax.ShapeDtypeStruct((full, w), bf16) for w in widths]
    chunks = 2 * pieces
    dma = pltpu.SemaphoreType.DMA
    scratch = (
        [pltpu.VMEM((full, w), f32) for w in widths]
        + [pltpu.VMEM((2, groups - 1, rows, w), f32) for w in widths]
        + [pltpu.VMEM((rows, w), f32) for w in widths] * 3
        + [pltpu.VMEM((full, w), bf16) for w in widths]
        + [pltpu.VMEM((groups, 8, 128), f32), pltpu.VMEM((shards, 8, 128), f32)]
        + [dma((groups, 2)), dma((2, 3)), dma((chunks, 3)), dma((2, groups, chunks))]
        + [dma((2, groups - 1, chunks))] * 2
        + [dma((groups,))] * 2
        + [dma((shards,))] * 2
        + [dma((2, groups, chunks))] * 2
    )
    outs = pl.pallas_call(
        functools.partial(kernel, groups, shards, float(count), pieces),
        out_shape=out_shape,
        in_specs=[pl.BlockSpec(memory_space=pltpu.HBM)] * 8,
        out_specs=[pl.BlockSpec(memory_space=pltpu.HBM)] * 8,
        scratch_shapes=scratch,
        compiler_params=pltpu.CompilerParams(
            collective_id=0, has_side_effects=True, vmem_limit_bytes=64 * 1024 * 1024
        ),
    )(*operands)
    return tuple(a[None] for a in copy_out(outs))


def solution(mesh):
    grads = P("group", "shard", None, None)
    state = P("shard", "group", None)
    gathered = P("shard", None, None)
    return jax.shard_map(
        functools.partial(body, mesh.shape["group"], mesh.shape["shard"]),
        mesh=mesh,
        in_specs=(grads,) * 2 + (state,) * 6,
        out_specs=(state,) * 6 + (gathered,) * 2,
        check_vma=False,
    )
```

```python
import functools

import jax
import jax.numpy as jnp
from jax import lax
from jax.experimental import pallas as pl
from jax.experimental.pallas import tpu as pltpu
from jax.sharding import PartitionSpec as P

beta_first = 0.9
beta_second = 0.95
learn_rate = 0.01
decay_rate = 0.1
epsilon = 1e-08
correct_first = 1.0 - 0.9**40
correct_second = 1.0 - 0.95**40

MESH = pl.DeviceIdType.MESH


def adamw_step(params, mean, square, total, clip):
    grads = clip * total
    moment = beta_first * mean + (1.0 - beta_first) * grads
    variance = beta_second * square + (1.0 - beta_second) * grads * grads
    update = moment / correct_first / (jnp.sqrt(variance / correct_second) + epsilon)
    master = params - learn_rate * (update + decay_rate * params)
    return (master, moment, variance)


def squares_tile(total):
    rows, width = total.shape
    squared = total * total
    folded = squared[0:8]
    for row in range(8, rows, 8):
        folded = folded + squared[row : row + 8]
    tile = folded[:, 0:128]
    for column in range(128, width, 128):
        tile = tile + folded[:, column : column + 128]
    return tile


def kernel(
    groups,
    shards,
    count,
    pieces,
    entry_grads, exit_grads,
    entry_params, exit_params, entry_mean, exit_mean, entry_square, exit_square,
    entry_master, exit_master, entry_moment, exit_moment,
    entry_variance, exit_variance, entry_weights, exit_weights,
    entry_x, exit_x, entry_held, exit_held,
    entry_p, exit_p, entry_m, exit_m, entry_v, exit_v, entry_w, exit_w,
    group_tiles, shard_tiles,
    load_sem, state_sem, store_sem,
    sum_send, sum_recv, tile_send, tile_recv, shard_send, shard_recv,
    gather_send, gather_recv,
):
    me = lax.axis_index("group")
    shard = lax.axis_index("shard")
    kinds = 2
    grads = (entry_grads, exit_grads)
    x = (entry_x, exit_x)
    held = (entry_held, exit_held)
    states = ((entry_p, entry_m, entry_v), (exit_p, exit_m, exit_v))
    state_in = (
        (entry_params, entry_mean, entry_square),
        (exit_params, exit_mean, exit_square),
    )
    state_out = (
        (entry_master, entry_moment, entry_variance),
        (exit_master, exit_moment, exit_variance),
    )
    gathered = (entry_w, exit_w)
    weights = (entry_weights, exit_weights)
    rows = entry_p.shape[0]
    steps = groups - 1

    def row_block(index):
        return pl.ds(pl.multiple_of(index * rows, rows), rows)

    near = lax.select(me < groups // 2, 0, 1)

    def wanted(stream, step):
        return (groups - 1 - step) * (1 - stream) + step * stream

    def load(k, step):
        block = row_block(wanted(near, step))
        return pltpu.make_async_copy(grads[k].at[block], x[k].at[block], load_sem.at[step, k])

    for step in range(groups):
        for k in range(kinds):
            load(k, step).start()

    barrier = pltpu.get_barrier_semaphore()
    for offset in range(1, groups):
        pl.semaphore_signal(
            barrier, inc=1, device_id={"group": lax.rem(me + offset, groups)}, device_id_type=MESH
        )
    for offset in range(1, shards):
        pl.semaphore_signal(
            barrier, inc=1, device_id={"shard": lax.rem(shard + offset, shards)}, device_id_type=MESH
        )
    pl.semaphore_wait(barrier, groups - 1 + shards - 1)
    state_loads = [
        pltpu.make_async_copy(state_in[k][i], states[k][i], state_sem.at[k, i])
        for k in range(kinds)
        for i in range(3)
    ]
    for copy in state_loads:
        copy.start()

    height = rows // pieces
    chunks = kinds * pieces

    def place_in(stream):
        return me + stream * (groups - 1 - 2 * me)

    def peer_in(stream):
        return {"group": me + 1 - 2 * stream}

    def piece_of(block, piece):
        return pl.ds(pl.multiple_of(block * rows + piece * height, height), height)

    def slot_of(stream, step, chunk):
        k, piece = chunk // pieces, chunk % pieces
        return held[k].at[stream, step, slice(piece * height, (piece + 1) * height)]

    def sum_copy(stream, step, chunk, source):
        return pltpu.make_async_remote_copy(
            src_ref=source,
            dst_ref=slot_of(stream, step, chunk),
            send_sem=sum_send.at[stream, step, chunk],
            recv_sem=sum_recv.at[stream, step, chunk],
            device_id=peer_in(stream),
            device_id_type=MESH,
        )

    if groups == 4:
        is_end = (me == 0) | (me == 3)
        mirror = me // 2
        total = 2 * chunks

        def block(j):
            return j + mirror * (3 - 2 * j)

        inwards = {"group": me + 1 - 2 * mirror}
        outwards = {"group": me - 1 + 2 * mirror}

        def line_copy(source, send, lane, step, chunk, peer):
            return pltpu.make_async_remote_copy(
                src_ref=source,
                dst_ref=slot_of(lane, step, chunk),
                send_sem=sum_send.at[send, step, chunk],
                recv_sem=sum_recv.at[lane, step, chunk],
                device_id=peer,
                device_id_type=MESH,
            )

        def end_copy(n):
            step, chunk = n // chunks, n % chunks
            source = x[chunk // pieces].at[piece_of(block(3 - step), chunk % pieces)]
            return line_copy(source, 0, 0, step, chunk, inwards)

        def across_copy(n):
            step, chunk = n // chunks, n % chunks
            return line_copy(slot_of(0, step, chunk), 0, 1, step, chunk, inwards)

        def back_copy(n):
            step, chunk = n // chunks, n % chunks
            return line_copy(slot_of(1, step, chunk), 1, 1, step, chunk, outwards)

        def shard_copy(offset):
            return pltpu.make_async_remote_copy(
                src_ref=shard_tiles.at[shard],
                dst_ref=shard_tiles.at[shard],
                send_sem=shard_send.at[offset],
                recv_sem=shard_recv.at[offset],
                device_id={"shard": lax.rem(shard + offset, shards)},
                device_id_type=MESH,
            )

        def tile_copy(offset):
            return pltpu.make_async_remote_copy(
                src_ref=group_tiles.at[me],
                dst_ref=group_tiles.at[me],
                send_sem=tile_send.at[offset],
                recv_sem=tile_recv.at[offset],
                device_id={"group": lax.rem(me + offset, groups)},
                device_id_type=MESH,
            )

        @pl.when(is_end)
        def _():
            lag = 8
            shard_tiles[shard] = jnp.zeros((8, 128), jnp.float32)
            for n in range(total + max(chunks, lag)):
                if n == 0:
                    load(0, 0).wait()
                if n == 1:
                    for step in range(groups):
                        for k in range(kinds):
                            if (step, k) != (0, 0):
                                load(k, step).wait()
                if n < total + chunks:
                    if n >= 2:
                        end_copy(n - 2).wait_send()
                    end_copy(n).start()
                m = n - lag
                if 0 <= m < total:
                    step, chunk = m // chunks, m % chunks
                    k, place = chunk // pieces, piece_of(block(step), chunk % pieces)
                    back_copy(m).wait_recv()
                    summed = x[k][place] + slot_of(1, step, chunk)[...]
                    if step == 0:
                        x[k][place] = summed
                    shard_tiles[shard] += squares_tile(summed)
                if m == total - 1:
                    for offset in range(1, shards):
                        shard_copy(offset).start()
            for offset in range(1, shards):
                shard_copy(offset).wait_recv()
            group_tiles[me] = jnp.sum(shard_tiles[...], axis=0)
            for offset in range(1, groups):
                tile_copy(offset).start()

        @pl.when(jnp.logical_not(is_end))
        def _():
            for step in range(groups):
                for k in range(kinds):
                    load(k, step).wait()
            for n in range(total + 1):
                if n < total:
                    step, chunk = n // chunks, n % chunks
                    k, place = chunk // pieces, piece_of(block(3 - step), chunk % pieces)
                    end_copy(n).wait_recv()
                    slot_of(0, step, chunk)[...] += x[k][place]
                    across_copy(n).start()
                if n >= 1:
                    step, chunk = (n - 1) // chunks, (n - 1) % chunks
                    k, place = chunk // pieces, piece_of(block(step), chunk % pieces)
                    across_copy(n - 1).wait_recv()
                    slot_of(1, step, chunk)[...] += x[k][place]
                    back_copy(n - 1).start()

        for copy in state_loads:
            copy.wait()
        for source in (0, 3):

            @pl.when(me != source)
            def _(source=source):
                tile_copy(lax.rem(me - source + groups, groups)).wait_recv()

        norm_tiles = jnp.stack([group_tiles[0], group_tiles[3]])
    else:
        @pl.when((me == 0) | (me == groups - 1))
        def _():
            copies = []
            for step in range(steps):
                for chunk in range(chunks):
                    k, piece = chunk // pieces, chunk % pieces
                    if piece == 0:
                        load(k, step).wait()
                    source = x[k].at[piece_of(wanted(near, step), piece)]
                    copies.append(sum_copy(near, step, chunk, source))
                    if len(copies) > 2:
                        copies[-3].wait_send()
                    copies[-1].start()
            for copy in copies[-2:]:
                copy.wait_send()

        @pl.when((me > 0) & (me < groups - 1))
        def _():
            for step in range(steps):
                for k in range(kinds):
                    load(k, step).wait()

        for k in range(kinds):
            load(k, steps).wait()

        own = row_block(me)
        for step in range(steps):
            target = groups - 1 - step
            for stream in (near, 1 - near):
                place = place_in(stream)
                for chunk in range(chunks):
                    k, piece = chunk // pieces, chunk % pieces

                    @pl.when((place > 0) & (place <= target))
                    def _(stream=stream, place=place, k=k, piece=piece, chunk=chunk):
                        slot = slot_of(stream, step, chunk)
                        copy = sum_copy(stream, step, chunk, slot)
                        copy.wait_recv()

                        @pl.when(place < target)
                        def _():
                            slot[...] += x[k][piece_of(wanted(stream, step), piece)]
                            copy.start()

                        @pl.when(place == target)
                        def _():
                            x[k][piece_of(me, piece)] += slot[...]

        group_tiles[me] = squares_tile(x[0][own]) + squares_tile(x[1][own])
        tile_copies = [
            pltpu.make_async_remote_copy(
                src_ref=group_tiles.at[me],
                dst_ref=group_tiles.at[me],
                send_sem=tile_send.at[offset],
                recv_sem=tile_recv.at[offset],
                device_id={"group": lax.rem(me + offset, groups)},
                device_id_type=MESH,
            )
            for offset in range(1, groups)
        ]
        for copy in tile_copies:
            copy.start()
        for copy in tile_copies:
            copy.wait_recv()
        shard_tiles[shard] = jnp.sum(group_tiles[...], axis=0)
        shard_copies = [
            pltpu.make_async_remote_copy(
                src_ref=shard_tiles.at[shard],
                dst_ref=shard_tiles.at[shard],
                send_sem=shard_send.at[offset],
                recv_sem=shard_recv.at[offset],
                device_id={"shard": lax.rem(shard + offset, shards)},
                device_id_type=MESH,
            )
            for offset in range(1, shards)
        ]
        for copy in shard_copies:
            copy.start()
        for copy in shard_copies:
            copy.wait_recv()
        norm_tiles = shard_tiles[...]
        for copy in state_loads:
            copy.wait()

    squares = jnp.sum(jnp.sum(norm_tiles, axis=0), keepdims=True)
    limit = jnp.sqrt(jnp.full((1, 1), count, jnp.float32))
    clip = jnp.minimum(jnp.float32(1.0), limit / (jnp.sqrt(squares) + 1e-06))

    parts = max(1, pieces // 2)
    tall = rows // parts
    batches = kinds * parts
    sums_in_batch = pieces // parts

    def gather_copy(stream, distance, batch, source_group):
        k, part = batch // parts, batch % parts
        place = pl.ds(pl.multiple_of(source_group * rows + part * tall, tall), tall)
        return pltpu.make_async_remote_copy(
            src_ref=gathered[k].at[place],
            dst_ref=gathered[k].at[place],
            send_sem=gather_send.at[stream, distance, batch],
            recv_sem=gather_recv.at[stream, distance, batch],
            device_id=peer_in(stream),
            device_id_type=MESH,
        )

    def has_next(stream):
        return me < groups - 1 if stream == 0 else me > 0

    for batch in range(batches):
        k, part = batch // parts, batch % parts
        rows_in = slice(part * tall, (part + 1) * tall)
        p, m, v = states[k]
        at = pl.ds(pl.multiple_of(me * rows + part * tall, tall), tall)
        if groups == 4:

            @pl.when(jnp.logical_not(is_end))
            def _():
                for chunk in range(batch * sums_in_batch, (batch + 1) * sums_in_batch):
                    end_copy(total + chunk).wait_recv()
                    x[k][piece_of(me, chunk % pieces)] = (
                        slot_of(1, 1, chunk)[...] + slot_of(0, 2, chunk)[...]
                    )

        master, moment, variance = adamw_step(p[rows_in], m[rows_in], v[rows_in], x[k][at], clip)
        gathered[k][at] = master.astype(jnp.bfloat16)
        for stream in range(2):

            @pl.when(has_next(stream))
            def _(stream=stream):
                gather_copy(stream, 0, batch, me).start()

        p[rows_in], m[rows_in], v[rows_in] = master, moment, variance

    stores = [
        pltpu.make_async_copy(states[k][i], state_out[k][i], store_sem.at[k, i])
        for k in range(kinds)
        for i in range(3)
    ]
    for copy in stores:
        copy.start()

    for distance in range(1, groups):
        for batch in range(batches):
            for stream in range(2):
                origin = me - distance if stream == 0 else me + distance

                @pl.when(origin >= 0 if stream == 0 else origin < groups)
                def _(stream=stream, origin=origin):
                    gather_copy(stream, distance - 1, batch, origin).wait_recv()

                    @pl.when(has_next(stream))
                    def _():
                        gather_copy(stream, distance, batch, origin).start()

    for k in range(kinds):
        stores.append(pltpu.make_async_copy(gathered[k], weights[k], store_sem.at[k, 3]))
        stores[-1].start()

    for distance in range(groups - 1):
        for batch in range(batches):
            for stream in range(2):
                origin = me - distance if stream == 0 else me + distance

                @pl.when(
                    has_next(stream) & (origin >= 0 if stream == 0 else origin < groups)
                )
                def _(stream=stream, origin=origin):
                    gather_copy(stream, distance, batch, origin).wait_send()

    if groups == 4:

        @pl.when(is_end)
        def _():
            for n in range(total + chunks - 2, total + chunks):
                end_copy(n).wait_send()
            for offset in range(1, shards):
                shard_copy(offset).wait_send()
            for offset in range(1, groups):
                tile_copy(offset).wait_send()

        @pl.when(jnp.logical_not(is_end))
        def _():
            for n in range(total):
                across_copy(n).wait_send()
                back_copy(n).wait_send()

    else:
        for step in range(steps):
            target = groups - 1 - step
            for stream in (near, 1 - near):
                place = place_in(stream)
                for chunk in range(chunks):

                    @pl.when((place > 0) & (place < target))
                    def _(stream=stream, chunk=chunk):
                        sum_copy(stream, step, chunk, slot_of(stream, step, chunk)).wait_send()

        for copy in tile_copies + shard_copies:
            copy.wait_send()
    for copy in stores:
        copy.wait()


def copy_kernel(*refs):
    count = (len(refs) - 2) // 3
    ins, outs, held = refs[:count], refs[count : 2 * count], refs[2 * count : 3 * count]
    load_sem, store_sem = refs[-2:]
    loads = [pltpu.make_async_copy(ins[i], held[i], load_sem.at[i]) for i in range(count)]
    stores = [pltpu.make_async_copy(held[i], outs[i], store_sem.at[i]) for i in range(count)]
    for copy in loads:
        copy.start()
    for load, store in zip(loads, stores):
        load.wait()
        store.start()
    for copy in stores:
        copy.wait()


def copy_out(arrays):
    moved = sum(2 * a.size * a.dtype.itemsize for a in arrays)
    return pl.pallas_call(
        copy_kernel,
        out_shape=[jax.ShapeDtypeStruct(a.shape, a.dtype) for a in arrays],
        in_specs=[pl.BlockSpec(memory_space=pltpu.HBM)] * len(arrays),
        out_specs=[pl.BlockSpec(memory_space=pltpu.HBM)] * len(arrays),
        scratch_shapes=[pltpu.VMEM(a.shape, a.dtype) for a in arrays]
        + [pltpu.SemaphoreType.DMA((len(arrays),))] * 2,
        cost_estimate=pl.CostEstimate(flops=0, bytes_accessed=moved, transcendentals=0),
        compiler_params=pltpu.CompilerParams(vmem_limit_bytes=64 * 1024 * 1024),
    )(*arrays)


def body(groups, shards, *args):
    entry_grads, exit_grads, *state = args
    full, entry_width = entry_grads.shape[2:]
    exit_width = exit_grads.shape[3]
    rows = full // groups
    pieces = max(1, rows // 16)
    count = full * (entry_width + exit_width) * shards
    widths = (entry_width, exit_width)
    f32, bf16 = jnp.float32, jnp.bfloat16
    operands = [entry_grads.reshape(full, entry_width), exit_grads.reshape(full, exit_width)]
    operands += [a.reshape(a.shape[1:]) for a in state]
    small = [jax.ShapeDtypeStruct((rows, w), f32) for w in widths]
    out_shape = small * 3 + [jax.ShapeDtypeStruct((full, w), bf16) for w in widths]
    chunks = 2 * pieces
    dma = pltpu.SemaphoreType.DMA
    scratch = (
        [pltpu.VMEM((full, w), f32) for w in widths]
        + [pltpu.VMEM((2, groups - 1, rows, w), f32) for w in widths]
        + [pltpu.VMEM((rows, w), f32) for w in widths] * 3
        + [pltpu.VMEM((full, w), bf16) for w in widths]
        + [pltpu.VMEM((groups, 8, 128), f32), pltpu.VMEM((shards, 8, 128), f32)]
        + [dma((groups, 2)), dma((2, 3)), dma((2, 4))]
        + [dma((2, groups - 1, chunks))] * 2
        + [dma((groups,))] * 2
        + [dma((shards,))] * 2
        + [dma((2, groups, chunks))] * 2
    )
    outs = pl.pallas_call(
        functools.partial(kernel, groups, shards, float(count), pieces),
        out_shape=out_shape,
        in_specs=[pl.BlockSpec(memory_space=pltpu.HBM)] * 8,
        out_specs=[pl.BlockSpec(memory_space=pltpu.HBM)] * 8,
        scratch_shapes=scratch,
        compiler_params=pltpu.CompilerParams(
            collective_id=0, has_side_effects=True, vmem_limit_bytes=64 * 1024 * 1024
        ),
    )(*operands)
    return tuple(a[None] for a in copy_out(outs))


def solution(mesh):
    grads = P("group", "shard", None, None)
    state = P("shard", "group", None)
    gathered = P("shard", None, None)
    return jax.shard_map(
        functools.partial(body, mesh.shape["group"], mesh.shape["shard"]),
        mesh=mesh,
        in_specs=(grads,) * 2 + (state,) * 6,
        out_specs=(state,) * 6 + (gathered,) * 2,
        check_vma=False,
    )
```

```python
import functools

import jax
import jax.numpy as jnp
from jax import lax
from jax.experimental import pallas as pl
from jax.experimental.pallas import tpu as pltpu
from jax.sharding import PartitionSpec as P

beta_first = 0.9
beta_second = 0.95
learn_rate = 0.01
decay_rate = 0.1
epsilon = 1e-08
correct_first = 1.0 - 0.9**40
correct_second = 1.0 - 0.95**40

MESH = pl.DeviceIdType.MESH


def adamw_step(params, mean, square, total, clip):
    grads = clip * total
    moment = beta_first * mean + (1.0 - beta_first) * grads
    variance = beta_second * square + (1.0 - beta_second) * grads * grads
    update = moment / correct_first / (jnp.sqrt(variance / correct_second) + epsilon)
    master = params - learn_rate * (update + decay_rate * params)
    return (master, moment, variance)


def squares_tile(total):
    rows, width = total.shape
    squared = total * total
    folded = squared[0:8]
    for row in range(8, rows, 8):
        folded = folded + squared[row : row + 8]
    tile = folded[:, 0:128]
    for column in range(128, width, 128):
        tile = tile + folded[:, column : column + 128]
    return tile


def kernel(
    groups,
    shards,
    count,
    pieces,
    entry_grads, exit_grads,
    entry_params, exit_params, entry_mean, exit_mean, entry_square, exit_square,
    entry_master, exit_master, entry_moment, exit_moment,
    entry_variance, exit_variance, entry_weights, exit_weights,
    entry_x, exit_x, entry_held, exit_held,
    entry_p, exit_p, entry_m, exit_m, entry_v, exit_v, entry_w, exit_w,
    group_tiles, shard_tiles,
    load_sem, state_sem, store_sem,
    sum_send, sum_recv, tile_send, tile_recv, shard_send, shard_recv,
    gather_send, gather_recv,
):
    me = lax.axis_index("group")
    shard = lax.axis_index("shard")
    kinds = 2
    grads = (entry_grads, exit_grads)
    x = (entry_x, exit_x)
    held = (entry_held, exit_held)
    states = ((entry_p, entry_m, entry_v), (exit_p, exit_m, exit_v))
    state_in = (
        (entry_params, entry_mean, entry_square),
        (exit_params, exit_mean, exit_square),
    )
    state_out = (
        (entry_master, entry_moment, entry_variance),
        (exit_master, exit_moment, exit_variance),
    )
    gathered = (entry_w, exit_w)
    weights = (entry_weights, exit_weights)
    rows = entry_p.shape[0]
    steps = groups - 1

    def row_block(index):
        return pl.ds(pl.multiple_of(index * rows, rows), rows)

    near = lax.select(me < groups // 2, 0, 1)

    def wanted(stream, step):
        return (groups - 1 - step) * (1 - stream) + step * stream

    def load(k, step):
        block = row_block(wanted(near, step))
        return pltpu.make_async_copy(grads[k].at[block], x[k].at[block], load_sem.at[step, k])

    for step in range(groups):
        for k in range(kinds):
            load(k, step).start()

    barrier = pltpu.get_barrier_semaphore()
    for offset in range(1, groups):
        pl.semaphore_signal(
            barrier, inc=1, device_id={"group": lax.rem(me + offset, groups)}, device_id_type=MESH
        )
    for offset in range(1, shards):
        pl.semaphore_signal(
            barrier, inc=1, device_id={"shard": lax.rem(shard + offset, shards)}, device_id_type=MESH
        )
    pl.semaphore_wait(barrier, groups - 1 + shards - 1)
    state_loads = [
        pltpu.make_async_copy(state_in[k][i], states[k][i], state_sem.at[k, i])
        for k in range(kinds)
        for i in range(3)
    ]
    for copy in state_loads:
        copy.start()

    height = rows // pieces
    chunks = kinds * pieces

    def place_in(stream):
        return me + stream * (groups - 1 - 2 * me)

    def peer_in(stream):
        return {"group": me + 1 - 2 * stream}

    def piece_of(block, piece):
        return pl.ds(pl.multiple_of(block * rows + piece * height, height), height)

    def slot_of(stream, step, chunk):
        k, piece = chunk // pieces, chunk % pieces
        return held[k].at[stream, step, slice(piece * height, (piece + 1) * height)]

    def sum_copy(stream, step, chunk, source):
        return pltpu.make_async_remote_copy(
            src_ref=source,
            dst_ref=slot_of(stream, step, chunk),
            send_sem=sum_send.at[stream, step, chunk],
            recv_sem=sum_recv.at[stream, step, chunk],
            device_id=peer_in(stream),
            device_id_type=MESH,
        )

    if groups == 4:
        is_end = (me == 0) | (me == 3)
        mirror = me // 2
        total = 2 * chunks
        window = min(6, chunks)

        def block(j):
            return j + mirror * (3 - 2 * j)

        inwards = {"group": me + 1 - 2 * mirror}
        outwards = {"group": me - 1 + 2 * mirror}

        def line_copy(source, send, lane, step, chunk, peer):
            return pltpu.make_async_remote_copy(
                src_ref=source,
                dst_ref=slot_of(lane, step, chunk),
                send_sem=sum_send.at[send, step, chunk],
                recv_sem=sum_recv.at[lane, step, chunk],
                device_id=peer,
                device_id_type=MESH,
            )

        def end_copy(n):
            step, chunk = n // chunks, n % chunks
            source = x[chunk // pieces].at[piece_of(block(3 - step), chunk % pieces)]
            return line_copy(source, 0, 0, step, chunk, inwards)

        def across_copy(n):
            step, chunk = n // chunks, n % chunks
            return line_copy(slot_of(0, step, chunk), 0, 1, step, chunk, inwards)

        def back_copy(n):
            step, chunk = n // chunks, n % chunks
            return line_copy(slot_of(1, step, chunk), 1, 1, step, chunk, outwards)

        def shard_copy(offset):
            return pltpu.make_async_remote_copy(
                src_ref=shard_tiles.at[shard],
                dst_ref=shard_tiles.at[shard],
                send_sem=shard_send.at[offset],
                recv_sem=shard_recv.at[offset],
                device_id={"shard": lax.rem(shard + offset, shards)},
                device_id_type=MESH,
            )

        def tile_copy(offset):
            return pltpu.make_async_remote_copy(
                src_ref=group_tiles.at[me],
                dst_ref=group_tiles.at[me],
                send_sem=tile_send.at[offset],
                recv_sem=tile_recv.at[offset],
                device_id={"group": lax.rem(me + offset, groups)},
                device_id_type=MESH,
            )

        @pl.when(is_end)
        def _():
            lag = 8
            shard_tiles[shard] = jnp.zeros((8, 128), jnp.float32)
            for n in range(total + max(chunks, lag)):
                if n == 0:
                    load(0, 0).wait()
                if n == 1:
                    for step in range(groups):
                        for k in range(kinds):
                            if (step, k) != (0, 0):
                                load(k, step).wait()
                if n < total + chunks:
                    if n >= window:
                        end_copy(n - window).wait_send()
                    end_copy(n).start()
                m = n - lag
                if 0 <= m < total:
                    step, chunk = m // chunks, m % chunks
                    k, place = chunk // pieces, piece_of(block(step), chunk % pieces)
                    back_copy(m).wait_recv()
                    summed = x[k][place] + slot_of(1, step, chunk)[...]
                    if step == 0:
                        x[k][place] = summed
                    shard_tiles[shard] += squares_tile(summed)
                if m == total - 1:
                    for offset in range(1, shards):
                        shard_copy(offset).start()
            for offset in range(1, shards):
                shard_copy(offset).wait_recv()
            group_tiles[me] = jnp.sum(shard_tiles[...], axis=0)
            for offset in range(1, groups):
                tile_copy(offset).start()

        @pl.when(jnp.logical_not(is_end))
        def _():
            for step in range(groups):
                for k in range(kinds):
                    load(k, step).wait()
            for n in range(total + 1):
                if n < total:
                    step, chunk = n // chunks, n % chunks
                    k, place = chunk // pieces, piece_of(block(3 - step), chunk % pieces)
                    end_copy(n).wait_recv()
                    slot_of(0, step, chunk)[...] += x[k][place]
                    across_copy(n).start()
                if n >= 1:
                    step, chunk = (n - 1) // chunks, (n - 1) % chunks
                    k, place = chunk // pieces, piece_of(block(step), chunk % pieces)
                    across_copy(n - 1).wait_recv()
                    slot_of(1, step, chunk)[...] += x[k][place]
                    back_copy(n - 1).start()

        for copy in state_loads:
            copy.wait()
        for source in (0, 3):

            @pl.when(me != source)
            def _(source=source):
                tile_copy(lax.rem(me - source + groups, groups)).wait_recv()

        norm_tiles = jnp.stack([group_tiles[0], group_tiles[3]])
    else:
        @pl.when((me == 0) | (me == groups - 1))
        def _():
            copies = []
            for step in range(steps):
                for chunk in range(chunks):
                    k, piece = chunk // pieces, chunk % pieces
                    if piece == 0:
                        load(k, step).wait()
                    source = x[k].at[piece_of(wanted(near, step), piece)]
                    copies.append(sum_copy(near, step, chunk, source))
                    if len(copies) > 2:
                        copies[-3].wait_send()
                    copies[-1].start()
            for copy in copies[-2:]:
                copy.wait_send()

        @pl.when((me > 0) & (me < groups - 1))
        def _():
            for step in range(steps):
                for k in range(kinds):
                    load(k, step).wait()

        for k in range(kinds):
            load(k, steps).wait()

        own = row_block(me)
        for step in range(steps):
            target = groups - 1 - step
            for stream in (near, 1 - near):
                place = place_in(stream)
                for chunk in range(chunks):
                    k, piece = chunk // pieces, chunk % pieces

                    @pl.when((place > 0) & (place <= target))
                    def _(stream=stream, place=place, k=k, piece=piece, chunk=chunk):
                        slot = slot_of(stream, step, chunk)
                        copy = sum_copy(stream, step, chunk, slot)
                        copy.wait_recv()

                        @pl.when(place < target)
                        def _():
                            slot[...] += x[k][piece_of(wanted(stream, step), piece)]
                            copy.start()

                        @pl.when(place == target)
                        def _():
                            x[k][piece_of(me, piece)] += slot[...]

        group_tiles[me] = squares_tile(x[0][own]) + squares_tile(x[1][own])
        tile_copies = [
            pltpu.make_async_remote_copy(
                src_ref=group_tiles.at[me],
                dst_ref=group_tiles.at[me],
                send_sem=tile_send.at[offset],
                recv_sem=tile_recv.at[offset],
                device_id={"group": lax.rem(me + offset, groups)},
                device_id_type=MESH,
            )
            for offset in range(1, groups)
        ]
        for copy in tile_copies:
            copy.start()
        for copy in tile_copies:
            copy.wait_recv()
        shard_tiles[shard] = jnp.sum(group_tiles[...], axis=0)
        shard_copies = [
            pltpu.make_async_remote_copy(
                src_ref=shard_tiles.at[shard],
                dst_ref=shard_tiles.at[shard],
                send_sem=shard_send.at[offset],
                recv_sem=shard_recv.at[offset],
                device_id={"shard": lax.rem(shard + offset, shards)},
                device_id_type=MESH,
            )
            for offset in range(1, shards)
        ]
        for copy in shard_copies:
            copy.start()
        for copy in shard_copies:
            copy.wait_recv()
        norm_tiles = shard_tiles[...]
        for copy in state_loads:
            copy.wait()

    squares = jnp.sum(jnp.sum(norm_tiles, axis=0), keepdims=True)
    limit = jnp.sqrt(jnp.full((1, 1), count, jnp.float32))
    clip = jnp.minimum(jnp.float32(1.0), limit / (jnp.sqrt(squares) + 1e-06))

    parts = max(1, pieces // 2)
    tall = rows // parts
    batches = kinds * parts
    sums_in_batch = pieces // parts

    def gather_copy(stream, distance, batch, source_group):
        k, part = batch // parts, batch % parts
        place = pl.ds(pl.multiple_of(source_group * rows + part * tall, tall), tall)
        return pltpu.make_async_remote_copy(
            src_ref=gathered[k].at[place],
            dst_ref=gathered[k].at[place],
            send_sem=gather_send.at[stream, distance, batch],
            recv_sem=gather_recv.at[stream, distance, batch],
            device_id=peer_in(stream),
            device_id_type=MESH,
        )

    def has_next(stream):
        return me < groups - 1 if stream == 0 else me > 0

    for batch in range(batches):
        k, part = batch // parts, batch % parts
        rows_in = slice(part * tall, (part + 1) * tall)
        p, m, v = states[k]
        at = pl.ds(pl.multiple_of(me * rows + part * tall, tall), tall)
        if groups == 4:

            @pl.when(jnp.logical_not(is_end))
            def _():
                for chunk in range(batch * sums_in_batch, (batch + 1) * sums_in_batch):
                    end_copy(total + chunk).wait_recv()
                    x[k][piece_of(me, chunk % pieces)] = (
                        slot_of(1, 1, chunk)[...] + slot_of(0, 2, chunk)[...]
                    )

        master, moment, variance = adamw_step(p[rows_in], m[rows_in], v[rows_in], x[k][at], clip)
        gathered[k][at] = master.astype(jnp.bfloat16)
        for stream in range(2):

            @pl.when(has_next(stream))
            def _(stream=stream):
                gather_copy(stream, 0, batch, me).start()

        p[rows_in], m[rows_in], v[rows_in] = master, moment, variance

    stores = [
        pltpu.make_async_copy(states[k][i], state_out[k][i], store_sem.at[k, i])
        for k in range(kinds)
        for i in range(3)
    ]
    for copy in stores:
        copy.start()

    for distance in range(1, groups):
        for batch in range(batches):
            for stream in range(2):
                origin = me - distance if stream == 0 else me + distance

                @pl.when(origin >= 0 if stream == 0 else origin < groups)
                def _(stream=stream, origin=origin):
                    gather_copy(stream, distance - 1, batch, origin).wait_recv()

                    @pl.when(has_next(stream))
                    def _():
                        gather_copy(stream, distance, batch, origin).start()

    for k in range(kinds):
        stores.append(pltpu.make_async_copy(gathered[k], weights[k], store_sem.at[k, 3]))
        stores[-1].start()

    for distance in range(groups - 1):
        for batch in range(batches):
            for stream in range(2):
                origin = me - distance if stream == 0 else me + distance

                @pl.when(
                    has_next(stream) & (origin >= 0 if stream == 0 else origin < groups)
                )
                def _(stream=stream, origin=origin):
                    gather_copy(stream, distance, batch, origin).wait_send()

    if groups == 4:

        @pl.when(is_end)
        def _():
            for n in range(total + chunks - window, total + chunks):
                end_copy(n).wait_send()
            for offset in range(1, shards):
                shard_copy(offset).wait_send()
            for offset in range(1, groups):
                tile_copy(offset).wait_send()

        @pl.when(jnp.logical_not(is_end))
        def _():
            for n in range(total):
                across_copy(n).wait_send()
                back_copy(n).wait_send()

    else:
        for step in range(steps):
            target = groups - 1 - step
            for stream in (near, 1 - near):
                place = place_in(stream)
                for chunk in range(chunks):

                    @pl.when((place > 0) & (place < target))
                    def _(stream=stream, chunk=chunk):
                        sum_copy(stream, step, chunk, slot_of(stream, step, chunk)).wait_send()

        for copy in tile_copies + shard_copies:
            copy.wait_send()
    for copy in stores:
        copy.wait()


def copy_kernel(*refs):
    count = (len(refs) - 2) // 3
    ins, outs, held = refs[:count], refs[count : 2 * count], refs[2 * count : 3 * count]
    load_sem, store_sem = refs[-2:]
    loads = [pltpu.make_async_copy(ins[i], held[i], load_sem.at[i]) for i in range(count)]
    stores = [pltpu.make_async_copy(held[i], outs[i], store_sem.at[i]) for i in range(count)]
    for copy in loads:
        copy.start()
    for load, store in zip(loads, stores):
        load.wait()
        store.start()
    for copy in stores:
        copy.wait()


def copy_out(arrays):
    moved = sum(2 * a.size * a.dtype.itemsize for a in arrays)
    return pl.pallas_call(
        copy_kernel,
        out_shape=[jax.ShapeDtypeStruct(a.shape, a.dtype) for a in arrays],
        in_specs=[pl.BlockSpec(memory_space=pltpu.HBM)] * len(arrays),
        out_specs=[pl.BlockSpec(memory_space=pltpu.HBM)] * len(arrays),
        scratch_shapes=[pltpu.VMEM(a.shape, a.dtype) for a in arrays]
        + [pltpu.SemaphoreType.DMA((len(arrays),))] * 2,
        cost_estimate=pl.CostEstimate(flops=0, bytes_accessed=moved, transcendentals=0),
        compiler_params=pltpu.CompilerParams(vmem_limit_bytes=64 * 1024 * 1024),
    )(*arrays)


def body(groups, shards, *args):
    entry_grads, exit_grads, *state = args
    full, entry_width = entry_grads.shape[2:]
    exit_width = exit_grads.shape[3]
    rows = full // groups
    pieces = max(1, rows // 16)
    count = full * (entry_width + exit_width) * shards
    widths = (entry_width, exit_width)
    f32, bf16 = jnp.float32, jnp.bfloat16
    operands = [entry_grads.reshape(full, entry_width), exit_grads.reshape(full, exit_width)]
    operands += [a.reshape(a.shape[1:]) for a in state]
    small = [jax.ShapeDtypeStruct((rows, w), f32) for w in widths]
    out_shape = small * 3 + [jax.ShapeDtypeStruct((full, w), bf16) for w in widths]
    chunks = 2 * pieces
    dma = pltpu.SemaphoreType.DMA
    scratch = (
        [pltpu.VMEM((full, w), f32) for w in widths]
        + [pltpu.VMEM((2, groups - 1, rows, w), f32) for w in widths]
        + [pltpu.VMEM((rows, w), f32) for w in widths] * 3
        + [pltpu.VMEM((full, w), bf16) for w in widths]
        + [pltpu.VMEM((groups, 8, 128), f32), pltpu.VMEM((shards, 8, 128), f32)]
        + [dma((groups, 2)), dma((2, 3)), dma((2, 4))]
        + [dma((2, groups - 1, chunks))] * 2
        + [dma((groups,))] * 2
        + [dma((shards,))] * 2
        + [dma((2, groups, chunks))] * 2
    )
    outs = pl.pallas_call(
        functools.partial(kernel, groups, shards, float(count), pieces),
        out_shape=out_shape,
        in_specs=[pl.BlockSpec(memory_space=pltpu.HBM)] * 8,
        out_specs=[pl.BlockSpec(memory_space=pltpu.HBM)] * 8,
        scratch_shapes=scratch,
        compiler_params=pltpu.CompilerParams(
            collective_id=0, has_side_effects=True, vmem_limit_bytes=64 * 1024 * 1024
        ),
    )(*operands)
    return tuple(a[None] for a in copy_out(outs))


def solution(mesh):
    grads = P("group", "shard", None, None)
    state = P("shard", "group", None)
    gathered = P("shard", None, None)
    return jax.shard_map(
        functools.partial(body, mesh.shape["group"], mesh.shape["shard"]),
        mesh=mesh,
        in_specs=(grads,) * 2 + (state,) * 6,
        out_specs=(state,) * 6 + (gathered,) * 2,
        check_vma=False,
    )
```

```python
import functools

import jax
import jax.numpy as jnp
from jax import lax
from jax.experimental import pallas as pl
from jax.experimental.pallas import tpu as pltpu
from jax.sharding import PartitionSpec as P

beta_first = 0.9
beta_second = 0.95
learn_rate = 0.01
decay_rate = 0.1
epsilon = 1e-08
correct_first = 1.0 - 0.9**40
correct_second = 1.0 - 0.95**40

MESH = pl.DeviceIdType.MESH


def adamw_step(params, mean, square, total, clip):
    grads = clip * total
    moment = beta_first * mean + (1.0 - beta_first) * grads
    variance = beta_second * square + (1.0 - beta_second) * grads * grads
    update = moment / correct_first / (jnp.sqrt(variance / correct_second) + epsilon)
    master = params - learn_rate * (update + decay_rate * params)
    return (master, moment, variance)


def squares_tile(total):
    rows, width = total.shape
    squared = total * total
    folded = squared[0:8]
    for row in range(8, rows, 8):
        folded = folded + squared[row : row + 8]
    tile = folded[:, 0:128]
    for column in range(128, width, 128):
        tile = tile + folded[:, column : column + 128]
    return tile


def kernel(
    groups,
    shards,
    count,
    pieces,
    entry_grads, exit_grads,
    entry_params, exit_params, entry_mean, exit_mean, entry_square, exit_square,
    entry_master, exit_master, entry_moment, exit_moment,
    entry_variance, exit_variance, entry_weights, exit_weights,
    entry_x, exit_x, entry_held, exit_held,
    entry_p, exit_p, entry_m, exit_m, entry_v, exit_v, entry_w, exit_w,
    group_tiles, shard_tiles,
    load_sem, state_sem, store_sem,
    sum_send, sum_recv, tile_send, tile_recv, shard_send, shard_recv,
    gather_send, gather_recv,
):
    me = lax.axis_index("group")
    shard = lax.axis_index("shard")
    kinds = 2
    grads = (entry_grads, exit_grads)
    x = (entry_x, exit_x)
    held = (entry_held, exit_held)
    states = ((entry_p, entry_m, entry_v), (exit_p, exit_m, exit_v))
    state_in = (
        (entry_params, entry_mean, entry_square),
        (exit_params, exit_mean, exit_square),
    )
    state_out = (
        (entry_master, entry_moment, entry_variance),
        (exit_master, exit_moment, exit_variance),
    )
    gathered = (entry_w, exit_w)
    weights = (entry_weights, exit_weights)
    rows = entry_p.shape[0]
    steps = groups - 1

    def row_block(index):
        return pl.ds(pl.multiple_of(index * rows, rows), rows)

    near = lax.select(me < groups // 2, 0, 1)

    def wanted(stream, step):
        return (groups - 1 - step) * (1 - stream) + step * stream

    def load(k, step):
        block = row_block(wanted(near, step))
        return pltpu.make_async_copy(grads[k].at[block], x[k].at[block], load_sem.at[step, k])

    for step in range(groups):
        for k in range(kinds):
            load(k, step).start()

    barrier = pltpu.get_barrier_semaphore()
    for offset in range(1, groups):
        pl.semaphore_signal(
            barrier, inc=1, device_id={"group": lax.rem(me + offset, groups)}, device_id_type=MESH
        )
    for offset in range(1, shards):
        pl.semaphore_signal(
            barrier, inc=1, device_id={"shard": lax.rem(shard + offset, shards)}, device_id_type=MESH
        )
    pl.semaphore_wait(barrier, groups - 1 + shards - 1)
    state_loads = [
        pltpu.make_async_copy(state_in[k][i], states[k][i], state_sem.at[k, i])
        for k in range(kinds)
        for i in range(3)
    ]
    for copy in state_loads:
        copy.start()

    height = rows // pieces
    chunks = kinds * pieces

    def place_in(stream):
        return me + stream * (groups - 1 - 2 * me)

    def peer_in(stream):
        return {"group": me + 1 - 2 * stream}

    def piece_of(block, piece):
        return pl.ds(pl.multiple_of(block * rows + piece * height, height), height)

    def slot_of(stream, step, chunk):
        k, piece = chunk // pieces, chunk % pieces
        return held[k].at[stream, step, slice(piece * height, (piece + 1) * height)]

    def sum_copy(stream, step, chunk, source):
        return pltpu.make_async_remote_copy(
            src_ref=source,
            dst_ref=slot_of(stream, step, chunk),
            send_sem=sum_send.at[stream, step, chunk],
            recv_sem=sum_recv.at[stream, step, chunk],
            device_id=peer_in(stream),
            device_id_type=MESH,
        )

    @pl.when((me == 0) | (me == groups - 1))
    def _():
        copies = []
        for step in range(steps):
            for chunk in range(chunks):
                k, piece = chunk // pieces, chunk % pieces
                if piece == 0:
                    load(k, step).wait()
                source = x[k].at[piece_of(wanted(near, step), piece)]
                copies.append(sum_copy(near, step, chunk, source))
                if len(copies) > 2:
                    copies[-3].wait_send()
                copies[-1].start()
        for copy in copies[-2:]:
            copy.wait_send()

    @pl.when((me > 0) & (me < groups - 1))
    def _():
        for step in range(steps):
            for k in range(kinds):
                load(k, step).wait()

    for k in range(kinds):
        load(k, steps).wait()

    own = row_block(me)
    for step in range(steps):
        target = groups - 1 - step
        for stream in (near, 1 - near):
            place = place_in(stream)
            for chunk in range(chunks):
                k, piece = chunk // pieces, chunk % pieces

                @pl.when((place > 0) & (place <= target))
                def _(stream=stream, place=place, k=k, piece=piece, chunk=chunk):
                    slot = slot_of(stream, step, chunk)
                    copy = sum_copy(stream, step, chunk, slot)
                    copy.wait_recv()

                    @pl.when(place < target)
                    def _():
                        slot[...] += x[k][piece_of(wanted(stream, step), piece)]
                        copy.start()

                    @pl.when(place == target)
                    def _():
                        x[k][piece_of(me, piece)] += slot[...]

    group_tiles[me] = squares_tile(x[0][own]) + squares_tile(x[1][own])
    tile_copies = [
        pltpu.make_async_remote_copy(
            src_ref=group_tiles.at[me],
            dst_ref=group_tiles.at[me],
            send_sem=tile_send.at[offset],
            recv_sem=tile_recv.at[offset],
            device_id={"group": lax.rem(me + offset, groups)},
            device_id_type=MESH,
        )
        for offset in range(1, groups)
    ]
    for copy in tile_copies:
        copy.start()
    for copy in state_loads:
        copy.wait()
    for copy in tile_copies:
        copy.wait_recv()
    shard_tiles[shard] = jnp.sum(group_tiles[...], axis=0)
    shard_copies = [
        pltpu.make_async_remote_copy(
            src_ref=shard_tiles.at[shard],
            dst_ref=shard_tiles.at[shard],
            send_sem=shard_send.at[offset],
            recv_sem=shard_recv.at[offset],
            device_id={"shard": lax.rem(shard + offset, shards)},
            device_id_type=MESH,
        )
        for offset in range(1, shards)
    ]
    for copy in shard_copies:
        copy.start()
    for copy in shard_copies:
        copy.wait_recv()
    squares = jnp.sum(jnp.sum(shard_tiles[...], axis=0), keepdims=True)
    limit = jnp.sqrt(jnp.full((1, 1), count, jnp.float32))
    clip = jnp.minimum(jnp.float32(1.0), limit / (jnp.sqrt(squares) + 1e-06))

    def gather_copy(stream, distance, chunk, source_group):
        k, piece = chunk // pieces, chunk % pieces
        block = gathered[k].at[piece_of(source_group, piece)]
        return pltpu.make_async_remote_copy(
            src_ref=block,
            dst_ref=block,
            send_sem=gather_send.at[stream, distance, chunk],
            recv_sem=gather_recv.at[stream, distance, chunk],
            device_id=peer_in(stream),
            device_id_type=MESH,
        )

    def has_next(stream):
        return me < groups - 1 if stream == 0 else me > 0

    for chunk in range(chunks):
        k, piece = chunk // pieces, chunk % pieces
        part = slice(piece * height, (piece + 1) * height)
        p, m, v = states[k]
        at = piece_of(me, piece)
        master, moment, variance = adamw_step(p[part], m[part], v[part], x[k][at], clip)
        gathered[k][at] = master.astype(jnp.bfloat16)
        for stream in range(2):

            @pl.when(has_next(stream))
            def _(stream=stream):
                if chunk >= 2:
                    gather_copy(stream, 0, chunk - 2, me).wait_send()
                gather_copy(stream, 0, chunk, me).start()

        p[part], m[part], v[part] = master, moment, variance

    stores = [
        pltpu.make_async_copy(states[k][i], state_out[k][i], store_sem.at[k, i])
        for k in range(kinds)
        for i in range(3)
    ]
    for copy in stores:
        copy.start()

    for distance in range(1, groups):
        for chunk in range(chunks):
            for stream in range(2):
                origin = me - distance if stream == 0 else me + distance

                @pl.when(origin >= 0 if stream == 0 else origin < groups)
                def _(stream=stream, origin=origin):
                    gather_copy(stream, distance - 1, chunk, origin).wait_recv()

                    @pl.when(has_next(stream))
                    def _():
                        gather_copy(stream, distance, chunk, origin).start()

    for k in range(kinds):
        stores.append(pltpu.make_async_copy(gathered[k], weights[k], store_sem.at[k, 3]))
        stores[-1].start()

    for distance in range(groups - 1):
        for chunk in range(0 if distance else chunks - 2, chunks):
            for stream in range(2):
                origin = me - distance if stream == 0 else me + distance

                @pl.when(
                    has_next(stream) & (origin >= 0 if stream == 0 else origin < groups)
                )
                def _(stream=stream, origin=origin):
                    gather_copy(stream, distance, chunk, origin).wait_send()

    for step in range(steps):
        target = groups - 1 - step
        for stream in (near, 1 - near):
            place = place_in(stream)
            for chunk in range(chunks):

                @pl.when((place > 0) & (place < target))
                def _(stream=stream, chunk=chunk):
                    sum_copy(stream, step, chunk, slot_of(stream, step, chunk)).wait_send()

    for copy in tile_copies + shard_copies:
        copy.wait_send()
    for copy in stores:
        copy.wait()


def copy_kernel(*refs):
    count = (len(refs) - 2) // 3
    ins, outs, held = refs[:count], refs[count : 2 * count], refs[2 * count : 3 * count]
    load_sem, store_sem = refs[-2:]
    loads = [pltpu.make_async_copy(ins[i], held[i], load_sem.at[i]) for i in range(count)]
    stores = [pltpu.make_async_copy(held[i], outs[i], store_sem.at[i]) for i in range(count)]
    for copy in loads:
        copy.start()
    for load, store in zip(loads, stores):
        load.wait()
        store.start()
    for copy in stores:
        copy.wait()


def copy_out(arrays):
    moved = sum(2 * a.size * a.dtype.itemsize for a in arrays)
    return pl.pallas_call(
        copy_kernel,
        out_shape=[jax.ShapeDtypeStruct(a.shape, a.dtype) for a in arrays],
        in_specs=[pl.BlockSpec(memory_space=pltpu.HBM)] * len(arrays),
        out_specs=[pl.BlockSpec(memory_space=pltpu.HBM)] * len(arrays),
        scratch_shapes=[pltpu.VMEM(a.shape, a.dtype) for a in arrays]
        + [pltpu.SemaphoreType.DMA((len(arrays),))] * 2,
        cost_estimate=pl.CostEstimate(flops=0, bytes_accessed=moved, transcendentals=0),
        compiler_params=pltpu.CompilerParams(vmem_limit_bytes=64 * 1024 * 1024),
    )(*arrays)


def body(groups, shards, *args):
    entry_grads, exit_grads, *state = args
    full, entry_width = entry_grads.shape[2:]
    exit_width = exit_grads.shape[3]
    rows = full // groups
    pieces = max(1, rows // 32)
    count = full * (entry_width + exit_width) * shards
    widths = (entry_width, exit_width)
    f32, bf16 = jnp.float32, jnp.bfloat16
    operands = [entry_grads.reshape(full, entry_width), exit_grads.reshape(full, exit_width)]
    operands += [a.reshape(a.shape[1:]) for a in state]
    small = [jax.ShapeDtypeStruct((rows, w), f32) for w in widths]
    out_shape = small * 3 + [jax.ShapeDtypeStruct((full, w), bf16) for w in widths]
    chunks = 2 * pieces
    dma = pltpu.SemaphoreType.DMA
    scratch = (
        [pltpu.VMEM((full, w), f32) for w in widths]
        + [pltpu.VMEM((2, groups - 1, rows, w), f32) for w in widths]
        + [pltpu.VMEM((rows, w), f32) for w in widths] * 3
        + [pltpu.VMEM((full, w), bf16) for w in widths]
        + [pltpu.VMEM((groups, 8, 128), f32), pltpu.VMEM((shards, 8, 128), f32)]
        + [dma((groups, 2)), dma((2, 3)), dma((2, 4))]
        + [dma((2, groups - 1, chunks))] * 2
        + [dma((groups,))] * 2
        + [dma((shards,))] * 2
        + [dma((2, groups, chunks))] * 2
    )
    outs = pl.pallas_call(
        functools.partial(kernel, groups, shards, float(count), pieces),
        out_shape=out_shape,
        in_specs=[pl.BlockSpec(memory_space=pltpu.HBM)] * 8,
        out_specs=[pl.BlockSpec(memory_space=pltpu.HBM)] * 8,
        scratch_shapes=scratch,
        compiler_params=pltpu.CompilerParams(
            collective_id=0, has_side_effects=True, vmem_limit_bytes=64 * 1024 * 1024
        ),
    )(*operands)
    return tuple(a[None] for a in copy_out(outs))


def solution(mesh):
    grads = P("group", "shard", None, None)
    state = P("shard", "group", None)
    gathered = P("shard", None, None)
    return jax.shard_map(
        functools.partial(body, mesh.shape["group"], mesh.shape["shard"]),
        mesh=mesh,
        in_specs=(grads,) * 2 + (state,) * 6,
        out_specs=(state,) * 6 + (gathered,) * 2,
        check_vma=False,
    )
```
